32 devices in a mesh: row: 16 (over z, y, core), col: 2 (over x).
Axes of the slice: x: 2, y: 2, z: 4, core: 2. Of those that a mesh axis runs over, the one named last changes fastest.
Arguments:
- alignment: bfloat16 [64, 768, 256], P('row', 'col'), may hold values from -10 to 10
- alignment_norm_gain: float32 [256], replicated, may hold values from 0.1 to 1.9
- alignment_norm_bias: float32 [256], replicated, may hold values from -1.75 to 1.75
- projection_weight: bfloat16 [256, 64], replicated, may hold values from -0.375 to 0.375
- projection_bias_pair: float32 [64], replicated, may hold values from -3 to 3
- w_out: bfloat16 [1024, 128], replicated, may hold values from -0.1875 to 0.1875
- b_out: float32 [128], replicated, may hold values from -1.75 to 1.75
- pair_gain: float32 [128], replicated, may hold values from 0.1 to 1.9
- pair_bias: float32 [128], replicated, may hold values from -1.75 to 1.75
- w_up: bfloat16 [128, 512], replicated, may hold values from -0.5 to 0.5
- b_up: float32 [512], replicated, may hold values from -1.75 to 1.75
- w_down: bfloat16 [512, 128], replicated, may hold values from -0.25 to 0.25
- b_down: float32 [128], replicated, may hold values from -1.75 to 1.75
Outputs:
- pair_out: bfloat16 [768, 768, 128], P('row', 'col')
The draws below stay inside these ranges and needn't reach their ends.
All inputs are finite; a program needn't handle non-finite values.
Results may differ from the reference program's by a relative error of at most 0.0052.
Values may be sent and summed in bfloat16 or wider, within the bound.
No kernel may reach another device: no remote copies, remote signals or barrier semaphores. Data moves between devices by JAX's collectives and lax.ppermute only.
A program may use at most 64 MiB of HBM per device.

```python
import jax
import jax.numpy as jnp
from jax import lax

CM = 256
C = 32
CZ = 128
CT = 512
I_DEV = 48
L = 768
S = 64


def draw_alignment(key, part):
    common_key, noise_key = jax.random.split(jax.random.fold_in(key, 11))
    common = jax.random.normal(common_key, (1, L, CM), jnp.float32)
    noise_part = jax.random.normal(noise_key, (S, L, CM), jnp.float32)
    values = jnp.clip(common + noise_part, -10.0, 10.0)
    return values.astype(jnp.bfloat16)


def centred(rng, dims, spread, bound, kind=jnp.bfloat16):
    drawn = jax.random.normal(rng, dims, jnp.float32) * spread
    return jnp.minimum(jnp.maximum(drawn, -bound), bound).astype(kind)


def setup_inputs(seed: int = 0) -> dict:
    keys = jax.random.split(jax.random.key(seed), 14)
    alignment = draw_alignment(jax.random.fold_in(keys[13], 71), 0)
    alignment_norm_gain = jnp.clip(1.0 + 0.18 * jax.random.normal(keys[1], (CM,), jnp.float32), 0.1, 1.9)
    alignment_norm_bias = centred(keys[2], (CM,), 0.3, 1.75, jnp.float32)
    projection_weight = centred(keys[3], (CM, 2 * C), CM ** -0.5, 0.375)
    projection_bias_pair = centred(keys[4], (2 * C,), 0.5, 3.0, jnp.float32)
    w_out = centred(keys[5], (C * C, CZ), (C * C) ** -0.5, 0.1875)
    b_out = centred(keys[6], (CZ,), 0.3, 1.75, jnp.float32)
    pair_gain = jnp.clip(1.0 + 0.18 * jax.random.normal(keys[7], (CZ,), jnp.float32), 0.1, 1.9)
    pair_bias = centred(keys[8], (CZ,), 0.3, 1.75, jnp.float32)
    w_up = centred(keys[9], (CZ, CT), CZ ** -0.5, 0.5)
    b_up = centred(keys[10], (CT,), 0.3, 1.75, jnp.float32)
    w_down = centred(keys[11], (CT, CZ), CT ** -0.5, 0.25)
    b_down = centred(keys[12], (CZ,), 0.3, 1.75, jnp.float32)
    return {"alignment": alignment, "alignment_norm_gain": alignment_norm_gain, "alignment_norm_bias": alignment_norm_bias, "projection_weight": projection_weight, "projection_bias_pair": projection_bias_pair, "w_out": w_out, "b_out": b_out, "pair_gain": pair_gain, "pair_bias": pair_bias, "w_up": w_up, "b_up": b_up, "w_down": w_down, "b_down": b_down}


EPSILON = 1e-05

def layer_norm(values, gain_vec, bias_vec):
    average = lax.optimization_barrier(jnp.mean(values, axis=-1, keepdims=True))
    centered = values - average
    variance = lax.optimization_barrier(jnp.mean(centered * centered, axis=-1, keepdims=True))
    return centered * lax.rsqrt(variance + EPSILON) * gain_vec.astype(jnp.float32) + bias_vec.astype(jnp.float32)

def project(rows_in, alignment_norm_gain, alignment_norm_bias, projection_weight, projection_bias_pair):
    normed = layer_norm(rows_in.astype(jnp.float32), alignment_norm_gain, alignment_norm_bias).astype(jnp.bfloat16)
    return (jnp.dot(normed, projection_weight, preferred_element_type=jnp.float32) + projection_bias_pair).astype(jnp.bfloat16)

def finish(forward, mirror, w_out, b_out, pair_gain, pair_bias, w_up, b_up, w_down, b_down):
    forward_z = jnp.dot(forward, w_out, preferred_element_type=jnp.float32) + b_out
    mirror_z = jnp.dot(mirror, w_out, preferred_element_type=jnp.float32) + b_out
    pair = jax.nn.relu(forward_z) + jax.nn.relu(mirror_z)
    normed = layer_norm(pair, pair_gain, pair_bias).astype(jnp.bfloat16)
    hidden = jax.nn.relu(jnp.dot(normed, w_up, preferred_element_type=jnp.float32) + b_up).astype(jnp.bfloat16)
    return (pair + jnp.dot(hidden, w_down, preferred_element_type=jnp.float32) + b_down).astype(jnp.bfloat16)

def reference(alignment, alignment_norm_gain, alignment_norm_bias, projection_weight, projection_bias_pair, w_out, b_out, pair_gain, pair_bias, w_up, b_up, w_down, b_down):
    projected = project(alignment.reshape(S * L, CM), alignment_norm_gain, alignment_norm_bias, projection_weight, projection_bias_pair).reshape(S, L, 2 * C)
    left_all = projected[:, :, :C].astype(jnp.float32)
    right_all = projected[:, :, C:].astype(jnp.float32)

    def pair_block(block_index):
        first_row = (block_index * I_DEV).astype(jnp.int32)
        left_rows = lax.dynamic_slice_in_dim(left_all, first_row, I_DEV, 1)
        right_rows = lax.dynamic_slice_in_dim(right_all, first_row, I_DEV, 1)
        forward = (jnp.einsum('sia,sjb->ijab', left_rows, right_all) / S).astype(jnp.bfloat16)
        mirror = (jnp.einsum('sja,sib->ijab', left_all, right_rows) / S).astype(jnp.bfloat16)
        result = finish(forward.reshape(I_DEV * L, C * C), mirror.reshape(I_DEV * L, C * C), w_out, b_out, pair_gain, pair_bias, w_up, b_up, w_down, b_down)
        return result.reshape(I_DEV, L, CZ)
    blocks_out = lax.map(pair_block, jnp.arange(L // I_DEV, dtype=jnp.int32))
    return blocks_out.reshape(L, L, CZ)
```

```python
import functools

import jax
import jax.numpy as jnp
from jax import lax
from jax.experimental import pallas as pl
from jax.experimental.pallas import tpu as pltpu
from jax.sharding import PartitionSpec as P

EPSILON = 1e-05
F32 = jnp.float32
BF16 = jnp.bfloat16


def norm_rows(values, gain, bias):
    average = jnp.mean(values, axis=-1, keepdims=True)
    centered = values - average
    variance = jnp.mean(centered * centered, axis=-1, keepdims=True)
    return centered * lax.rsqrt(variance + EPSILON) * gain + bias


def project_body(core_ref, x_ref, gain_ref, bias_ref, weight_ref, pbias_ref, out_ref):
    local, _, _ = x_ref.shape
    width = weight_ref.shape[1]
    group = 2 * local
    lanes = width * group
    first = core_ref[0] * local
    ch = lax.broadcasted_iota(jnp.int32, (width, lanes), 0)
    lane = lax.broadcasted_iota(jnp.int32, (width, lanes), 1)
    total = None
    for s in range(local):
        normed = norm_rows(x_ref[s].astype(F32), gain_ref[...], bias_ref[...]).astype(BF16)
        y = jnp.dot(normed, weight_ref[...], preferred_element_type=F32) + pbias_ref[...]
        spread = (lane == ch * group + (first + s)).astype(F32).astype(BF16)
        part = jnp.dot(y.astype(BF16), spread, preferred_element_type=F32)
        total = part if total is None else total + part
    half = lanes // 2
    out_ref[0] = total[:, :half].astype(BF16)
    out_ref[1] = total[:, half:].astype(BF16)


def project(core, x, gain, bias, weight, pbias):
    local, residues, _ = x.shape
    lanes = weight.shape[1] * local
    vmem = pl.BlockSpec(memory_space=pltpu.VMEM)
    return pl.pallas_call(
        project_body,
        in_specs=[pl.BlockSpec(memory_space=pltpu.SMEM)] + [vmem] * 5,
        out_specs=vmem,
        out_shape=jax.ShapeDtypeStruct((2, residues, lanes), BF16),
        compiler_params=pltpu.CompilerParams(vmem_limit_bytes=32 << 20),
    )(core, x, gain, bias, weight, pbias)


def pair_body(
    chips, rows_here, rows_ref, *refs
):
    cols = refs[:chips]
    (w_ref, b_out_ref, gain_ref, bias_ref, w_up_ref, b_up_ref, w_down_ref, b_down_ref) = refs[
        chips : chips + 8
    ]
    out_ref, col_scr, t_scr, z_scr = refs[chips + 8 :]
    part = cols[0].shape[2]
    depth = chips * part
    zc = out_ref.shape[2]
    group = part // (w_ref.shape[1] // (2 * zc))
    total = chips * group
    half = part // group

    @pl.when(pl.program_id(0) == 0)
    def _():
        for q in range(chips):
            for d in range(2):
                col_scr[d, :, q * part : (q + 1) * part] = cols[q][d]

    lhs = rows_ref[...].reshape(rows_here * total, rows_ref.shape[2])
    for d in range(2):
        for bp in range(half // 2):
            lane = (d * half + 2 * bp) * zc
            t = jnp.dot(lhs, w_ref[:, lane : lane + 2 * zc], preferred_element_type=F32)
            t = t.reshape(rows_here * chips, group, 2 * zc)
            t = jnp.concatenate([t[:, :, :zc], t[:, :, zc:]], axis=1).astype(BF16)
            t = t.reshape(rows_here, chips, 2 * group, zc)
            for g in range(rows_here):
                for q in range(chips):
                    k = q * part + bp * 2 * group
                    t_scr[d, g // 2, k : k + 2 * group, (g % 2) * zc : (g % 2 + 1) * zc] = t[g, q]
    for p in range(rows_here // 2):
        for d in range(2):
            z_scr[d, p] = jnp.dot(col_scr[d], t_scr[d, p], preferred_element_type=F32)
    for g in range(rows_here):
        lanes = slice((g % 2) * zc, (g % 2 + 1) * zc)
        forward = z_scr[0, g // 2, :, lanes] * (1.0 / total) + b_out_ref[...]
        mirror = z_scr[1, g // 2, :, lanes] * (1.0 / total) + b_out_ref[...]
        pair = jnp.maximum(forward, 0.0) + jnp.maximum(mirror, 0.0)
        normed = norm_rows(pair, gain_ref[...], bias_ref[...]).astype(BF16)
        hidden = jnp.dot(normed, w_up_ref[...], preferred_element_type=F32) + b_up_ref[...]
        hidden = jnp.maximum(hidden, 0.0).astype(BF16)
        update = jnp.dot(hidden, w_down_ref[...], preferred_element_type=F32)
        out_ref[g] = (pair + update + b_down_ref[...]).astype(BF16)


def pair_kernel(rows, cols, w, b_out, gain, bias, w_up, b_up, w_down, b_down):
    row_length, total, width = rows.shape
    chips = len(cols)
    _, column_length, part = cols[0].shape
    zc = w_down.shape[1]
    here = 4
    depth = chips * part

    def whole(a):
        return pl.BlockSpec(a.shape, lambda i: (0,) * a.ndim)

    rest = (w, b_out, gain, bias, w_up, b_up, w_down, b_down)
    return pl.pallas_call(
        functools.partial(pair_body, chips, here),
        grid=(row_length // here,),
        in_specs=[pl.BlockSpec((here, total, width), lambda i: (i, 0, 0))]
        + [whole(a) for a in cols]
        + [whole(a) for a in rest],
        out_specs=pl.BlockSpec((here, column_length, zc), lambda i: (i, 0, 0)),
        out_shape=jax.ShapeDtypeStruct((row_length, column_length, zc), BF16),
        scratch_shapes=[
            pltpu.VMEM((2, column_length, depth), BF16),
            pltpu.VMEM((2, here // 2, depth, 2 * zc), BF16),
            pltpu.VMEM((2, here // 2, column_length, 2 * zc), F32),
        ],
        compiler_params=pltpu.CompilerParams(vmem_limit_bytes=56 << 20),
    )(rows, *cols, *rest)


def chip_ring(chips):
    order = list(range(0, chips, 2)) + list(range(chips - 1, 0, -2))
    after = {order[i]: order[(i + 1) % chips] for i in range(chips)}
    before = {v: k for k, v in after.items()}
    return [
        (2 * q + core, 2 * (after if core == 0 else before)[q] + core)
        for q in range(chips)
        for core in range(2)
    ]


def shards(
    alignment,
    alignment_norm_gain,
    alignment_norm_bias,
    projection_weight,
    projection_bias_pair,
    w_out,
    b_out,
    pair_gain,
    pair_bias,
    w_up,
    b_up,
    w_down,
    b_down,
):
    local, column_length, _ = alignment.shape
    width = projection_weight.shape[1]
    half = width // 2
    row_count = lax.axis_size("row")
    col_count = lax.axis_size("col")
    row_length = column_length * col_count // row_count
    chips = row_count // 2
    zc = w_out.shape[1]
    row_index = lax.axis_index("row")
    col_index = lax.axis_index("col")
    core = row_index % 2

    def swap(a):
        return lax.ppermute(a, "row", [(r, r ^ 1) for r in range(row_count)])

    ring = chip_ring(chips)

    weight = jnp.concatenate([projection_weight[:, half:], projection_weight[:, :half]], axis=1)
    pbias = jnp.concatenate([projection_bias_pair[half:], projection_bias_pair[:half]])
    mine = project(
        core.reshape(1),
        alignment,
        alignment_norm_gain[None],
        alignment_norm_bias[None],
        weight,
        pbias[None],
    )
    own = mine + swap(mine)
    right, left = own[0], own[1]
    cols = [own]
    others = []
    for _ in range(chips // 2 - 1):
        right = lax.ppermute(right, "row", ring)
        left = lax.ppermute(left, "row", ring)
        cols.append(jnp.stack([right, left]))
        others.append(jnp.stack([swap(right), swap(left)]))
    far = lax.ppermute(jnp.where(core == 0, right, left), "row", ring)
    far_other = swap(far)
    far = jnp.stack([jnp.where(core == 0, far, far_other), jnp.where(core == 0, far_other, far)])
    cols = cols + others + [far]

    per_col = column_length // row_length
    start = (row_index % per_col) * row_length
    source = row_index // per_col
    block = jnp.stack([lax.dynamic_slice_in_dim(c, start, row_length, 1) for c in cols])
    if col_count == 2:
        there = lax.ppermute(block, "col", [(0, 1), (1, 0)])
        block = jnp.where(source == col_index, block, there)
    else:
        block = lax.dynamic_index_in_dim(lax.all_gather(block, "col"), source, 0, False)
    group = 2 * local
    rows = block.reshape(chips, 2, row_length, half, group).transpose(2, 0, 4, 1, 3)
    rows = rows.reshape(row_length, chips * group, width)

    w3 = w_out.reshape(half, half, zc)
    w_forward = w3.reshape(half, half * zc)
    w_mirror = w3.transpose(1, 0, 2).reshape(half, half * zc)
    zero = jnp.zeros_like(w_forward)
    w = jnp.concatenate(
        [
            jnp.concatenate([zero, w_mirror], axis=1),
            jnp.concatenate([w_forward, zero], axis=1),
        ],
        axis=0,
    )
    return pair_kernel(
        rows,
        cols,
        w,
        b_out[None],
        pair_gain[None],
        pair_bias[None],
        w_up,
        b_up[None],
        w_down,
        b_down[None],
    )


def solution(mesh):
    return jax.shard_map(
        shards,
        mesh=mesh,
        in_specs=(P("row", "col", None),) + (P(),) * 12,
        out_specs=P("row", "col", None),
        check_vma=False,
    )
```

```python
import functools

import jax
import jax.numpy as jnp
from jax import lax
from jax.experimental import pallas as pl
from jax.experimental.pallas import tpu as pltpu
from jax.sharding import PartitionSpec as P

EPSILON = 1e-05
F32 = jnp.float32
BF16 = jnp.bfloat16
F8 = jnp.float8_e4m3fn


def norm_rows(values, gain, bias):
    average = jnp.mean(values, axis=-1, keepdims=True)
    centered = values - average
    variance = jnp.mean(centered * centered, axis=-1, keepdims=True)
    return centered * lax.rsqrt(variance + EPSILON) * gain + bias


def project_body(core_ref, x_ref, gain_ref, bias_ref, weight_ref, pbias_ref, out_ref):
    local, _, _ = x_ref.shape
    width = weight_ref.shape[1]
    group = 2 * local
    lanes = width * group
    first = core_ref[0] * local
    ch = lax.broadcasted_iota(jnp.int32, (width, lanes), 0)
    lane = lax.broadcasted_iota(jnp.int32, (width, lanes), 1)
    total = None
    for s in range(local):
        normed = norm_rows(x_ref[s].astype(F32), gain_ref[...], bias_ref[...]).astype(BF16)
        y = jnp.dot(normed, weight_ref[...], preferred_element_type=F32) + pbias_ref[...]
        spread = (lane == ch * group + (first + s)).astype(F32).astype(BF16)
        part = jnp.dot(y.astype(BF16), spread, preferred_element_type=F32)
        total = part if total is None else total + part
    half = lanes // 2
    out_ref[0] = total[:, :half].astype(BF16)
    out_ref[1] = total[:, half:].astype(BF16)


def project(core, x, gain, bias, weight, pbias):
    local, residues, _ = x.shape
    lanes = weight.shape[1] * local
    vmem = pl.BlockSpec(memory_space=pltpu.VMEM)
    return pl.pallas_call(
        project_body,
        in_specs=[pl.BlockSpec(memory_space=pltpu.SMEM)] + [vmem] * 5,
        out_specs=vmem,
        out_shape=jax.ShapeDtypeStruct((2, residues, lanes), BF16),
        compiler_params=pltpu.CompilerParams(vmem_limit_bytes=32 << 20),
    )(core, x, gain, bias, weight, pbias)


def power_of_two(largest):
    scale = jnp.ones_like(largest)
    inverse = jnp.ones_like(largest)
    for k in (32, 16, 8, 4, 2, 1):
        fits = largest * (scale * float(2**k)) <= 448.0
        scale = jnp.where(fits, scale * float(2**k), scale)
        inverse = jnp.where(fits, inverse * float(2.0**-k), inverse)
    return scale, inverse


def split_weight_body(total, w_ref, w8_ref, undo_ref, scr):
    half = w8_ref.shape[0] // 8
    zc = w_ref.shape[1]
    scr[...] = w_ref[...].astype(F32)
    scale, inverse = power_of_two(jnp.max(jnp.abs(scr[...]), axis=0, keepdims=True))
    undo_ref[...] = inverse * (1.0 / total)
    zero = jnp.zeros((4 * half, half * zc), w8_ref.dtype)
    w8_ref[4 * half :, : half * zc] = zero
    w8_ref[: 4 * half, half * zc :] = zero
    for d in range(2):
        for k in range(half):
            if d == 0:
                block = scr[pl.ds(k, half, stride=half), :]
            else:
                block = scr[k * half : (k + 1) * half, :]
            block = block * scale
            high = block.astype(w8_ref.dtype)
            low = (block - high.astype(F32)).astype(w8_ref.dtype)
            lanes = slice((d * half + k) * zc, (d * half + k + 1) * zc)
            row = d * 4 * half
            w8_ref[row : row + half, lanes] = high
            w8_ref[row + half : row + 2 * half, lanes] = high
            w8_ref[row + 2 * half : row + 3 * half, lanes] = low
            w8_ref[row + 3 * half : row + 4 * half, lanes] = low


def split_weight(w_out, half, total):
    zc = w_out.shape[1]
    vmem = pl.BlockSpec(memory_space=pltpu.VMEM)
    return pl.pallas_call(
        functools.partial(split_weight_body, total),
        in_specs=[vmem],
        out_specs=[vmem, vmem],
        out_shape=[
            jax.ShapeDtypeStruct((8 * half, 2 * half * zc), F8),
            jax.ShapeDtypeStruct((1, zc), F32),
        ],
        scratch_shapes=[pltpu.VMEM(w_out.shape, F32)],
        compiler_params=pltpu.CompilerParams(vmem_limit_bytes=32 << 20),
    )(w_out)


def prepare_rows(chips, group, row_refs, undo_ref, y_scr, lhs_scr, undo_scr):
    row_length = row_refs[0].shape[2]
    part = row_refs[0].shape[3]
    half = part // group
    lanes = 4 * half
    k = lax.broadcasted_iota(jnp.int32, (part, lanes), 0)
    lane = lax.broadcasted_iota(jnp.int32, (part, lanes), 1)
    offset = k - lax.rem(lane, half) * group
    count = chips * row_length
    for side in range(2):
        x = jnp.concatenate(
            [r[q, 1 - side] for r in row_refs for q in range(r.shape[0])], axis=0
        )
        for s in range(group):
            pick = jnp.where(offset == s, 1.0, 0.0).astype(BF16)
            y_scr[side, pl.ds(s, count, stride=group), :] = jnp.dot(
                x, pick, preferred_element_type=F32
            )
        largest = None
        for q in range(chips):
            y = y_scr[side, q * row_length * group : (q + 1) * row_length * group, :]
            m = jnp.max(jnp.abs(y).reshape(row_length, group, lanes), axis=1)
            largest = m if largest is None else jnp.maximum(largest, m)
        largest = jnp.max(largest, axis=-1, keepdims=True)
        scale, inverse = power_of_two(jnp.broadcast_to(largest, (row_length, lanes)))
        undo_scr[side] = inverse * undo_ref[...]
        spread = jnp.broadcast_to(scale[:, None, :], (row_length, group, lanes)).reshape(
            row_length * group, lanes
        )
        here = lax.broadcasted_iota(jnp.int32, (row_length * group, lanes), 1)
        is_high = lax.rem(lax.div(here, half), 2) == 0
        for q in range(chips):
            y = y_scr[side, q * row_length * group : (q + 1) * row_length * group, :] * spread
            high = y.astype(F8).astype(F32)
            both = jnp.where(is_high, high, y - high).astype(F8)
            lhs_scr[q, :, side * lanes : (side + 1) * lanes] = both


def pair_body(chips, here, group, row_parts, core_ref, *refs):
    row_refs = refs[:row_parts]
    refs = refs[row_parts:]
    own_ref, *col_refs = refs[: chips * 2 - 1]
    (w_ref, undo_ref, b_out_ref, gain_ref, bias_ref, w_up_ref, b_up_ref, w_down_ref, b_down_ref) = (
        refs[chips * 2 - 1 : chips * 2 + 8]
    )
    out_ref, col_scr, y_scr, lhs_scr, undo_scr, t_scr, z_scr = refs[chips * 2 + 8 :]
    part = own_ref.shape[2]
    zc = out_ref.shape[2]
    half = part // group
    step = pl.program_id(0)

    @pl.when(step == 0)
    def _():
        for d in range(2):
            col_scr[d, :, :part] = own_ref[d]
            for q in range(1, chips - 1):
                col_scr[d, :, q * part : (q + 1) * part] = col_refs[2 * (q - 1) + d][...]

        far = slice((chips - 1) * part, chips * part)
        far_here, far_there = col_refs[-2:]

        @pl.when(core_ref[0] == 0)
        def _():
            col_scr[0, :, far] = far_here[...]
            col_scr[1, :, far] = far_there[...]

        @pl.when(core_ref[0] != 0)
        def _():
            col_scr[0, :, far] = far_there[...]
            col_scr[1, :, far] = far_here[...]

        prepare_rows(chips, group, row_refs, undo_ref, y_scr, lhs_scr, undo_scr)

    rows = here * group
    lhs = lhs_scr[:, pl.ds(pl.multiple_of(step * rows, rows), rows), :].reshape(
        chips * rows, lhs_scr.shape[2]
    )
    for d in range(2):
        for bp in range(half // 2):
            lane = (d * half + 2 * bp) * zc
            t = jnp.dot(lhs, w_ref[:, lane : lane + 2 * zc], preferred_element_type=F32)
            t = t.reshape(chips * here, group, 2 * zc)
            t = jnp.concatenate([t[:, :, :zc], t[:, :, zc:]], axis=1).astype(BF16)
            t = t.reshape(chips, here, 2 * group, zc)
            for g in range(here):
                for q in range(chips):
                    k = q * part + bp * 2 * group
                    t_scr[d, g // 2, k : k + 2 * group, (g % 2) * zc : (g % 2 + 1) * zc] = t[q, g]
    for p in range(here // 2):
        for d in range(2):
            z_scr[d, p] = jnp.dot(col_scr[d], t_scr[d, p], preferred_element_type=F32)
    for g in range(here):
        lanes = slice((g % 2) * zc, (g % 2 + 1) * zc)
        undo = [undo_scr[d, pl.ds(step * here + g, 1), :] for d in range(2)]
        forward = z_scr[0, g // 2, :, lanes] * undo[0] + b_out_ref[...]
        mirror = z_scr[1, g // 2, :, lanes] * undo[1] + b_out_ref[...]
        pair = jnp.maximum(forward, 0.0) + jnp.maximum(mirror, 0.0)
        normed = norm_rows(pair, gain_ref[...], bias_ref[...]).astype(BF16)
        hidden = jnp.dot(normed, w_up_ref[...], preferred_element_type=F32) + b_up_ref[...]
        hidden = jnp.maximum(hidden, 0.0).astype(BF16)
        update = jnp.dot(hidden, w_down_ref[...], preferred_element_type=F32)
        out_ref[g] = (pair + update + b_down_ref[...]).astype(BF16)


def pair_kernel(core, group, rows, cols, rest):
    own = cols[0]
    _, column_length, part = own.shape
    chips = (len(cols) + 1) // 2
    row_length = rows[0].shape[2]
    zc = rest[2].shape[1]
    here = 4
    depth = chips * part
    lanes = 4 * part // group

    def whole(a):
        return pl.BlockSpec(a.shape, lambda i: (0,) * a.ndim)

    return pl.pallas_call(
        functools.partial(pair_body, chips, here, group, len(rows)),
        grid=(row_length // here,),
        in_specs=[pl.BlockSpec(memory_space=pltpu.SMEM)]
        + [whole(a) for a in (*rows, *cols, *rest)],
        out_specs=pl.BlockSpec((here, column_length, zc), lambda i: (i, 0, 0)),
        out_shape=jax.ShapeDtypeStruct((row_length, column_length, zc), BF16),
        scratch_shapes=[
            pltpu.VMEM((2, column_length, depth), BF16),
            pltpu.VMEM((2, chips * row_length * group, lanes), F32),
            pltpu.VMEM((chips, row_length * group, 2 * lanes), F8),
            pltpu.VMEM((2, row_length, zc), F32),
            pltpu.VMEM((2, here // 2, depth, 2 * zc), BF16),
            pltpu.VMEM((2, here // 2, column_length, 2 * zc), F32),
        ],
        compiler_params=pltpu.CompilerParams(vmem_limit_bytes=56 << 20),
    )(core, *rows, *cols, *rest)


def chip_ring(chips):
    order = list(range(0, chips, 2)) + list(range(chips - 1, 0, -2))
    after = {order[i]: order[(i + 1) % chips] for i in range(chips)}
    before = {v: k for k, v in after.items()}
    return [
        (2 * q + core, 2 * (after if core == 0 else before)[q] + core)
        for q in range(chips)
        for core in range(2)
    ]


def shards(
    alignment,
    alignment_norm_gain,
    alignment_norm_bias,
    projection_weight,
    projection_bias_pair,
    w_out,
    b_out,
    pair_gain,
    pair_bias,
    w_up,
    b_up,
    w_down,
    b_down,
):
    local, column_length, _ = alignment.shape
    width = projection_weight.shape[1]
    half = width // 2
    row_count = lax.axis_size("row")
    col_count = lax.axis_size("col")
    row_length = column_length * col_count // row_count
    chips = row_count // 2
    row_index = lax.axis_index("row")
    col_index = lax.axis_index("col")
    core = row_index % 2

    def swap(a):
        return lax.ppermute(a, "row", [(r, r ^ 1) for r in range(row_count)])

    ring = chip_ring(chips)

    weight = jnp.concatenate([projection_weight[:, half:], projection_weight[:, :half]], axis=1)
    pbias = jnp.concatenate([projection_bias_pair[half:], projection_bias_pair[:half]])
    mine = project(
        core.reshape(1),
        alignment,
        alignment_norm_gain[None],
        alignment_norm_bias[None],
        weight,
        pbias[None],
    )
    own = mine + swap(mine)

    per_col = column_length // row_length
    start = (row_index % per_col) * row_length
    source = row_index // per_col

    def exchange(pieces):
        block = jnp.stack(
            [
                jnp.stack([lax.dynamic_slice_in_dim(c, start, row_length, 0) for c in pair])
                for pair in pieces
            ]
        )
        if col_count == 2:
            there = lax.ppermute(block, "col", [(0, 1), (1, 0)])
            return jnp.where(source == col_index, block, there)
        return lax.dynamic_index_in_dim(lax.all_gather(block, "col"), source, 0, False)

    right, left = own[0], own[1]
    cols = [own]
    early = [(right, left)]
    late = []
    steps = chips // 2 - 1
    for d in range(steps):
        right = lax.ppermute(right, "row", ring)
        left = lax.ppermute(left, "row", ring)
        pieces = [(right, left), (swap(right), swap(left))]
        for pair in pieces:
            cols.extend(pair)
        (early if d < steps - 1 else late).extend(pieces)
    far = lax.ppermute(jnp.where(core == 0, right, left), "row", ring)
    far_other = swap(far)
    cols.extend([far, far_other])
    late.append((jnp.where(core == 0, far, far_other), jnp.where(core == 0, far_other, far)))
    rows = [exchange(early), exchange(late)]

    group = 2 * local
    w8, undo = split_weight(w_out, half, group * chips)
    rest = (w8, undo, b_out[None], pair_gain[None], pair_bias[None], w_up, b_up[None], w_down)
    return pair_kernel(core.reshape(1), group, rows, cols, rest + (b_down[None],))


def solution(mesh):
    return jax.shard_map(
        shards,
        mesh=mesh,
        in_specs=(P("row", "col", None),) + (P(),) * 12,
        out_specs=P("row", "col", None),
        check_vma=False,
    )
```

```python
import functools
import math

import jax
import jax.numpy as jnp
from jax import lax
from jax.experimental import pallas as pl
from jax.experimental.pallas import tpu as pltpu
from jax.sharding import PartitionSpec as P

EPSILON = 1e-05
F32 = jnp.float32
BF16 = jnp.bfloat16
F8 = jnp.float8_e4m3fn


def norm_rows(values, gain, bias):
    average = jnp.mean(values, axis=-1, keepdims=True)
    centered = values - average
    variance = jnp.mean(centered * centered, axis=-1, keepdims=True)
    return centered * lax.rsqrt(variance + EPSILON) * gain + bias


def project_body(core_ref, x_ref, gain_ref, bias_ref, weight_ref, pbias_ref, out_ref):
    local, _, _ = x_ref.shape
    width = weight_ref.shape[1]
    group = 2 * local
    lanes = width * group
    first = core_ref[0] * local
    ch = lax.rem(lax.broadcasted_iota(jnp.int32, (width, lanes), 0) + width // 2, width)
    lane = lax.broadcasted_iota(jnp.int32, (width, lanes), 1)
    total = None
    for s in range(local):
        normed = norm_rows(x_ref[s].astype(F32), gain_ref[...], bias_ref[...]).astype(BF16)
        y = jnp.dot(normed, weight_ref[...], preferred_element_type=F32) + pbias_ref[...]
        spread = (lane == ch * group + (first + s)).astype(F32).astype(BF16)
        part = jnp.dot(y.astype(BF16), spread, preferred_element_type=F32)
        total = part if total is None else total + part
    half = lanes // 2
    out_ref[0] = total[:, :half].astype(BF16)
    out_ref[1] = total[:, half:].astype(BF16)


def project(core, x, gain, bias, weight, pbias):
    local, residues, _ = x.shape
    lanes = weight.shape[1] * local
    vmem = pl.BlockSpec(memory_space=pltpu.VMEM)
    return pl.pallas_call(
        project_body,
        in_specs=[pl.BlockSpec(memory_space=pltpu.SMEM)] + [vmem] * 5,
        out_specs=vmem,
        out_shape=jax.ShapeDtypeStruct((2, residues, lanes), BF16),
        compiler_params=pltpu.CompilerParams(vmem_limit_bytes=32 << 20),
    )(core, x, gain, bias, weight, pbias)


def power_of_two(largest):
    scale = jnp.ones_like(largest)
    inverse = jnp.ones_like(largest)
    for k in (32, 16, 8, 4, 2, 1):
        fits = largest * (scale * float(2**k)) <= 448.0
        scale = jnp.where(fits, scale * float(2**k), scale)
        inverse = jnp.where(fits, inverse * float(2.0**-k), inverse)
    return scale, inverse


def split_weight_body(total, w_ref, w8_ref, undo_ref, scr):
    half = w8_ref.shape[0] // 8
    zc = w_ref.shape[1]
    scr[...] = w_ref[...].astype(F32)
    scale, inverse = power_of_two(jnp.max(jnp.abs(scr[...]), axis=0, keepdims=True))
    undo_ref[...] = inverse * (1.0 / total)
    zero = jnp.zeros((4 * half, half * zc), w8_ref.dtype)
    w8_ref[4 * half :, : half * zc] = zero
    w8_ref[: 4 * half, half * zc :] = zero
    for d in range(2):
        for k in range(half):
            if d == 0:
                block = scr[pl.ds(k, half, stride=half), :]
            else:
                block = scr[k * half : (k + 1) * half, :]
            block = block * scale
            high = block.astype(w8_ref.dtype)
            low = (block - high.astype(F32)).astype(w8_ref.dtype)
            lanes = slice((d * half + k) * zc, (d * half + k + 1) * zc)
            row = d * 4 * half
            w8_ref[row : row + half, lanes] = high
            w8_ref[row + half : row + 2 * half, lanes] = high
            w8_ref[row + 2 * half : row + 3 * half, lanes] = low
            w8_ref[row + 3 * half : row + 4 * half, lanes] = low


def split_weight(w_out, half, total):
    zc = w_out.shape[1]
    vmem = pl.BlockSpec(memory_space=pltpu.VMEM)
    return pl.pallas_call(
        functools.partial(split_weight_body, total),
        in_specs=[vmem],
        out_specs=[vmem, vmem],
        out_shape=[
            jax.ShapeDtypeStruct((8 * half, 2 * half * zc), F8),
            jax.ShapeDtypeStruct((1, zc), F32),
        ],
        scratch_shapes=[pltpu.VMEM(w_out.shape, F32)],
        compiler_params=pltpu.CompilerParams(vmem_limit_bytes=32 << 20),
    )(w_out)


def prepare_rows(chips, group, x_scr, undo_ref, y_scr, lhs_scr, undo_scr):
    row_length = x_scr.shape[1] // chips
    part = x_scr.shape[2]
    half = part // group
    lanes = 4 * half
    k = lax.broadcasted_iota(jnp.int32, (part, lanes), 0)
    lane = lax.broadcasted_iota(jnp.int32, (part, lanes), 1)
    offset = k - lax.rem(lane, half) * group
    count = chips * row_length
    for side in range(2):
        x = x_scr[1 - side]
        for s in range(group):
            pick = jnp.where(offset == s, 1.0, 0.0).astype(BF16)
            y_scr[side, pl.ds(s, count, stride=group), :] = jnp.dot(
                x, pick, preferred_element_type=F32
            )
        largest = None
        for q in range(chips):
            y = y_scr[side, q * row_length * group : (q + 1) * row_length * group, :]
            m = jnp.max(jnp.abs(y).reshape(row_length, group, lanes), axis=1)
            largest = m if largest is None else jnp.maximum(largest, m)
        largest = jnp.max(largest, axis=-1, keepdims=True)
        scale, inverse = power_of_two(jnp.broadcast_to(largest, (row_length, lanes)))
        undo_scr[side] = inverse * undo_ref[...]
        spread = jnp.broadcast_to(scale[:, None, :], (row_length, group, lanes)).reshape(
            row_length * group, lanes
        )
        here = lax.broadcasted_iota(jnp.int32, (row_length * group, lanes), 1)
        is_high = lax.rem(lax.div(here, half), 2) == 0
        for q in range(chips):
            y = y_scr[side, q * row_length * group : (q + 1) * row_length * group, :] * spread
            high = y.astype(F8).astype(F32)
            both = jnp.where(is_high, high, y - high).astype(F8)
            lhs_scr[q, :, side * lanes : (side + 1) * lanes] = both


def pair_body(chips, here, group, row_parts, place_ref, *refs):
    here_refs, there_refs = refs[:row_parts], refs[row_parts : 2 * row_parts]
    refs = refs[2 * row_parts :]
    own_ref, *col_refs = refs[: chips * 2 - 1]
    (w_ref, undo_ref, b_out_ref, gain_ref, bias_ref, w_up_ref, b_up_ref, w_down_ref, b_down_ref) = (
        refs[chips * 2 - 1 : chips * 2 + 8]
    )
    out_ref, col_scr, x_scr, y_scr, lhs_scr, undo_scr, t_scr, z_scr = refs[chips * 2 + 8 :]
    part = own_ref.shape[2]
    zc = out_ref.shape[2]
    half = part // group
    step = pl.program_id(0)

    @pl.when(step == 0)
    def _():
        for d in range(2):
            col_scr[d, :, :part] = own_ref[d]
            for q in range(1, chips - 1):
                col_scr[d, :, q * part : (q + 1) * part] = col_refs[2 * (q - 1) + d][...]

        far = slice((chips - 1) * part, chips * part)
        far_here, far_there = col_refs[-2:]

        @pl.when(place_ref[0] == 0)
        def _():
            col_scr[0, :, far] = far_here[...]
            col_scr[1, :, far] = far_there[...]

        @pl.when(place_ref[0] != 0)
        def _():
            col_scr[0, :, far] = far_there[...]
            col_scr[1, :, far] = far_here[...]

        def take(row_refs):
            blocks = [(r, q) for r in row_refs for q in range(r.shape[0])]
            for i, (r, q) in enumerate(blocks):
                for side in range(2):
                    x_scr[side, i * r.shape[2] : (i + 1) * r.shape[2], :] = r[q, side]

        @pl.when(place_ref[1] != 0)
        def _():
            take(here_refs)

        @pl.when(place_ref[1] == 0)
        def _():
            take(there_refs)

        prepare_rows(chips, group, x_scr, undo_ref, y_scr, lhs_scr, undo_scr)

    rows = here * group
    lhs = lhs_scr[:, pl.ds(pl.multiple_of(step * rows, rows), rows), :].reshape(
        chips * rows, lhs_scr.shape[2]
    )
    for d in range(2):
        for bp in range(half // 2):
            lane = (d * half + 2 * bp) * zc
            t = jnp.dot(lhs, w_ref[:, lane : lane + 2 * zc], preferred_element_type=F32)
            t = t.reshape(chips * here, group, 2 * zc)
            t = jnp.concatenate([t[:, :, :zc], t[:, :, zc:]], axis=1).astype(BF16)
            t = t.reshape(chips, here, 2 * group, zc)
            for g in range(here):
                for q in range(chips):
                    k = q * part + bp * 2 * group
                    t_scr[d, g // 2, k : k + 2 * group, (g % 2) * zc : (g % 2 + 1) * zc] = t[q, g]
    for p in range(here // 2):
        for d in range(2):
            z_scr[d, p] = jnp.dot(col_scr[d], t_scr[d, p], preferred_element_type=F32)
    for g in range(here):
        lanes = slice((g % 2) * zc, (g % 2 + 1) * zc)
        undo = [undo_scr[d, pl.ds(step * here + g, 1), :] for d in range(2)]
        forward = z_scr[0, g // 2, :, lanes] * undo[0] + b_out_ref[...]
        mirror = z_scr[1, g // 2, :, lanes] * undo[1] + b_out_ref[...]
        pair = jnp.maximum(forward, 0.0) + jnp.maximum(mirror, 0.0)
        normed = norm_rows(pair, gain_ref[...], bias_ref[...]).astype(BF16)
        hidden = jnp.dot(normed, w_up_ref[...], preferred_element_type=F32) + b_up_ref[...]
        hidden = jnp.maximum(hidden, 0.0).astype(BF16)
        update = jnp.dot(hidden, w_down_ref[...], preferred_element_type=F32)
        out_ref[g] = (pair + update + b_down_ref[...]).astype(BF16)


def pair_kernel(place, group, rows_here, rows_there, cols, rest):
    own = cols[0]
    _, column_length, part = own.shape
    chips = (len(cols) + 1) // 2
    row_length = rows_here[0].shape[2]
    zc = rest[2].shape[1]
    here = math.gcd(row_length, 8)
    depth = chips * part
    lanes = 4 * part // group

    def whole(a):
        return pl.BlockSpec(a.shape, lambda i: (0,) * a.ndim)

    return pl.pallas_call(
        functools.partial(pair_body, chips, here, group, len(rows_here)),
        grid=(row_length // here,),
        in_specs=[pl.BlockSpec(memory_space=pltpu.SMEM)]
        + [whole(a) for a in (*rows_here, *rows_there, *cols, *rest)],
        out_specs=pl.BlockSpec((here, column_length, zc), lambda i: (i, 0, 0)),
        out_shape=jax.ShapeDtypeStruct((row_length, column_length, zc), BF16),
        scratch_shapes=[
            pltpu.VMEM((2, column_length, depth), BF16),
            pltpu.VMEM((2, chips * row_length, part), BF16),
            pltpu.VMEM((2, chips * row_length * group, lanes), F32),
            pltpu.VMEM((chips, row_length * group, 2 * lanes), F8),
            pltpu.VMEM((2, row_length, zc), F32),
            pltpu.VMEM((2, here // 2, depth, 2 * zc), BF16),
            pltpu.VMEM((2, here // 2, column_length, 2 * zc), F32),
        ],
        compiler_params=pltpu.CompilerParams(vmem_limit_bytes=56 << 20),
    )(place, *rows_here, *rows_there, *cols, *rest)


def chip_ring(chips):
    order = list(range(0, chips, 2)) + list(range(chips - 1, 0, -2))
    after = {order[i]: order[(i + 1) % chips] for i in range(chips)}
    before = {v: k for k, v in after.items()}
    return [
        (2 * q + core, 2 * (after if core == 0 else before)[q] + core)
        for q in range(chips)
        for core in range(2)
    ]


def shards(
    alignment,
    alignment_norm_gain,
    alignment_norm_bias,
    projection_weight,
    projection_bias_pair,
    w_out,
    b_out,
    pair_gain,
    pair_bias,
    w_up,
    b_up,
    w_down,
    b_down,
):
    local, column_length, _ = alignment.shape
    width = projection_weight.shape[1]
    half = width // 2
    row_count = lax.axis_size("row")
    col_count = lax.axis_size("col")
    row_length = column_length * col_count // row_count
    chips = row_count // 2
    row_index = lax.axis_index("row")
    col_index = lax.axis_index("col")
    core = row_index % 2

    def swap(a):
        return lax.ppermute(a, "row", [(r, r ^ 1) for r in range(row_count)])

    ring = chip_ring(chips)

    mine = project(
        core.reshape(1),
        alignment,
        alignment_norm_gain[None],
        alignment_norm_bias[None],
        projection_weight,
        projection_bias_pair[None],
    )
    own = mine + swap(mine)

    per_col = column_length // row_length
    start = (row_index % per_col) * row_length
    source = row_index // per_col

    def cut(pieces, first):
        return jnp.stack(
            [
                jnp.stack([lax.dynamic_slice_in_dim(c, first, row_length, 0) for c in pair])
                for pair in pieces
            ]
        )

    def exchange(pieces):
        block = cut(pieces, start)
        if col_count == 2:
            return block, lax.ppermute(block, "col", [(0, 1), (1, 0)])
        block = lax.dynamic_index_in_dim(lax.all_gather(block, "col"), source, 0, False)
        return block, block

    right, left = own[0], own[1]
    cols = [own]
    early = [(right, left)]
    if col_count == 2:
        opposite = [row_count - 2 - r + 2 * (r % 2) for r in range(row_count)]
        target = row_count - 2 - row_index + 2 * core
        far_there = lax.ppermute(
            cut(early, (target % per_col) * row_length),
            ("row", "col"),
            [(2 * r + t // per_col, 2 * t + 1 - t // per_col) for r, t in enumerate(opposite)],
        )
    rows = []
    steps = chips // 2 - 1
    for d in range(steps):
        right = lax.ppermute(right, "row", ring)
        left = lax.ppermute(left, "row", ring)
        pieces = [(right, left), (swap(right), swap(left))]
        for pair in pieces:
            cols.extend(pair)
        early.extend(pieces)
        if d >= steps - 2:
            rows.append(exchange(early))
            early = []
        if d == 0:
            params = (w_out, b_out, pair_gain, pair_bias, w_up, b_up, w_down, b_down)
            *params, right, left = lax.optimization_barrier((*params, right, left))
    far = lax.ppermute(jnp.where(core == 0, right, left), "row", ring)
    far_other = swap(far)
    cols.extend([far, far_other])
    a = lax.dynamic_slice_in_dim(far, start, row_length, 0)
    b = lax.dynamic_slice_in_dim(far_other, start, row_length, 0)
    far_pair = (jnp.where(core == 0, a, b), jnp.where(core == 0, b, a))
    if col_count == 2:
        rows.append((jnp.stack(far_pair)[None], far_there))
    else:
        block = lax.all_gather(jnp.stack(far_pair)[None], "col")
        block = lax.dynamic_index_in_dim(block, source, 0, False)
        rows.append((block, block))

    group = 2 * local
    w_out, b_out, pair_gain, pair_bias, w_up, b_up, w_down, b_down = params
    w8, undo = split_weight(w_out, half, group * chips)
    rest = (w8, undo, b_out[None], pair_gain[None], pair_bias[None], w_up, b_up[None], w_down)
    place = jnp.stack([core, (source == col_index).astype(core.dtype)])
    return pair_kernel(
        place, group, [r[0] for r in rows], [r[1] for r in rows], cols, rest + (b_down[None],)
    )


def solution(mesh):
    return jax.shard_map(
        shards,
        mesh=mesh,
        in_specs=(P("row", "col", None),) + (P(),) * 12,
        out_specs=P("row", "col", None),
        check_vma=False,
    )
```

```python
import functools
import math

import jax
import jax.numpy as jnp
from jax import lax
from jax.experimental import pallas as pl
from jax.experimental.pallas import tpu as pltpu
from jax.sharding import PartitionSpec as P

EPSILON = 1e-05
F32 = jnp.float32
BF16 = jnp.bfloat16
F8 = jnp.float8_e4m3fn


def norm_rows(values, gain, bias):
    average = jnp.mean(values, axis=-1, keepdims=True)
    centered = values - average
    variance = jnp.mean(centered * centered, axis=-1, keepdims=True)
    return centered * lax.rsqrt(variance + EPSILON) * gain + bias


def project_body(core_ref, x_ref, gain_ref, bias_ref, weight_ref, pbias_ref, out_ref):
    local, _, _ = x_ref.shape
    width = weight_ref.shape[0]
    group = 2 * local
    lanes = width * group
    first = core_ref[0] * local
    ch = lax.rem(lax.broadcasted_iota(jnp.int32, (width, lanes), 0) + width // 2, width)
    lane = lax.broadcasted_iota(jnp.int32, (width, lanes), 1)
    total = None
    for s in range(local):
        normed = norm_rows(x_ref[s].astype(F32), gain_ref[...], bias_ref[...]).astype(BF16)
        y = lax.dot_general(
            normed, weight_ref[...], (((1,), (1,)), ((), ())), preferred_element_type=F32
        )
        y = y + pbias_ref[...]
        spread = (lane == ch * group + (first + s)).astype(F32).astype(BF16)
        part = jnp.dot(y.astype(BF16), spread, preferred_element_type=F32)
        total = part if total is None else total + part
    half = lanes // 2
    out_ref[0] = total[:, :half].astype(BF16)
    out_ref[1] = total[:, half:].astype(BF16)


def whole(a):
    return pl.BlockSpec(a.shape, lambda i: (0,) * len(a.shape))


def project(core, x, gain, bias, weight, pbias):
    local, residues, _ = x.shape
    lanes = weight.shape[0] * local
    out = jax.ShapeDtypeStruct((2, residues, lanes), BF16)
    return pl.pallas_call(
        project_body,
        grid=(1,),
        in_specs=[pl.BlockSpec(memory_space=pltpu.SMEM)]
        + [whole(a) for a in (x, gain, bias, weight, pbias)],
        out_specs=whole(out),
        out_shape=out,
        compiler_params=pltpu.CompilerParams(vmem_limit_bytes=32 << 20),
    )(core, x, gain, bias, weight, pbias)


def power_of_two(largest):
    scale = jnp.ones_like(largest)
    inverse = jnp.ones_like(largest)
    for k in (32, 16, 8, 4, 2, 1):
        fits = largest * (scale * float(2**k)) <= 448.0
        scale = jnp.where(fits, scale * float(2**k), scale)
        inverse = jnp.where(fits, inverse * float(2.0**-k), inverse)
    return scale, inverse


def split_weight_body(total, w_ref, w8_ref, undo_ref, scr):
    half = w8_ref.shape[0] // 8
    zc = w_ref.shape[1]
    scr[...] = w_ref[...].astype(F32)
    scale, inverse = power_of_two(jnp.max(jnp.abs(scr[...]), axis=0, keepdims=True))
    undo_ref[...] = inverse * (1.0 / total)
    zero = jnp.zeros((4 * half, half * zc), w8_ref.dtype)
    w8_ref[4 * half :, : half * zc] = zero
    w8_ref[: 4 * half, half * zc :] = zero
    for d in range(2):
        for k in range(half):
            if d == 0:
                block = scr[pl.ds(k, half, stride=half), :]
            else:
                block = scr[k * half : (k + 1) * half, :]
            block = block * scale
            high = block.astype(w8_ref.dtype)
            low = (block - high.astype(F32)).astype(w8_ref.dtype)
            lanes = slice((d * half + k) * zc, (d * half + k + 1) * zc)
            row = d * 4 * half
            w8_ref[row : row + half, lanes] = high
            w8_ref[row + half : row + 2 * half, lanes] = high
            w8_ref[row + 2 * half : row + 3 * half, lanes] = low
            w8_ref[row + 3 * half : row + 4 * half, lanes] = low


def split_weight(w_out, half, total):
    zc = w_out.shape[1]
    outs = [
        jax.ShapeDtypeStruct((8 * half, 2 * half * zc), F8),
        jax.ShapeDtypeStruct((1, zc), F32),
    ]
    return pl.pallas_call(
        functools.partial(split_weight_body, total),
        grid=(1,),
        in_specs=[whole(w_out)],
        out_specs=[whole(a) for a in outs],
        out_shape=outs,
        scratch_shapes=[pltpu.VMEM(w_out.shape, F32)],
        compiler_params=pltpu.CompilerParams(vmem_limit_bytes=32 << 20),
    )(w_out)


def prepare_rows(chips, group, x_scr, undo_ref, y_scr, lhs_scr, undo_scr):
    row_length = x_scr.shape[1] // chips
    part = x_scr.shape[2]
    half = part // group
    lanes = 4 * half
    k = lax.broadcasted_iota(jnp.int32, (part, lanes), 0)
    lane = lax.broadcasted_iota(jnp.int32, (part, lanes), 1)
    offset = k - lax.rem(lane, half) * group
    count = chips * row_length
    for side in range(2):
        x = x_scr[1 - side]
        for s in range(group):
            pick = jnp.where(offset == s, 1.0, 0.0).astype(BF16)
            y_scr[side, pl.ds(s, count, stride=group), :] = jnp.dot(
                x, pick, preferred_element_type=F32
            )
        largest = None
        for q in range(chips):
            y = y_scr[side, q * row_length * group : (q + 1) * row_length * group, :]
            m = jnp.max(jnp.abs(y).reshape(row_length, group, lanes), axis=1)
            largest = m if largest is None else jnp.maximum(largest, m)
        largest = jnp.max(largest, axis=-1, keepdims=True)
        scale, inverse = power_of_two(jnp.broadcast_to(largest, (row_length, lanes)))
        undo_scr[side] = inverse * undo_ref[...]
        spread = jnp.broadcast_to(scale[:, None, :], (row_length, group, lanes)).reshape(
            row_length * group, lanes
        )
        here = lax.broadcasted_iota(jnp.int32, (row_length * group, lanes), 1)
        is_high = lax.rem(lax.div(here, half), 2) == 0
        for q in range(chips):
            y = y_scr[side, q * row_length * group : (q + 1) * row_length * group, :] * spread
            high = y.astype(F8).astype(F32)
            both = jnp.where(is_high, high, y - high).astype(F8)
            lhs_scr[q, :, side * lanes : (side + 1) * lanes] = both


def pair_body(chips, here, group, row_parts, place_ref, *refs):
    here_refs, there_refs = refs[:row_parts], refs[row_parts : 2 * row_parts]
    refs = refs[2 * row_parts :]
    own_ref, *col_refs = refs[: chips * 2 - 1]
    (w_ref, undo_ref, b_out_ref, gain_ref, bias_ref, w_up_ref, b_up_ref, w_down_ref, b_down_ref) = (
        refs[chips * 2 - 1 : chips * 2 + 8]
    )
    out_ref, col_scr, x_scr, y_scr, lhs_scr, undo_scr, t_scr, z_scr = refs[chips * 2 + 8 :]
    part = own_ref.shape[2]
    zc = out_ref.shape[2]
    half = part // group
    step = pl.program_id(0)

    @pl.when(step == 0)
    def _():
        for d in range(2):
            col_scr[d, :, :part] = own_ref[d]
            for q in range(1, chips - 1):
                col_scr[d, :, q * part : (q + 1) * part] = col_refs[2 * (q - 1) + d][...]

        far = slice((chips - 1) * part, chips * part)
        far_here, far_there = col_refs[-2:]

        @pl.when(place_ref[0] == 0)
        def _():
            col_scr[0, :, far] = far_here[...]
            col_scr[1, :, far] = far_there[...]

        @pl.when(place_ref[0] != 0)
        def _():
            col_scr[0, :, far] = far_there[...]
            col_scr[1, :, far] = far_here[...]

        def take(row_refs):
            blocks = [(r, q) for r in row_refs for q in range(r.shape[0])]
            for i, (r, q) in enumerate(blocks):
                for side in range(2):
                    x_scr[side, i * r.shape[2] : (i + 1) * r.shape[2], :] = r[q, side]

        @pl.when(place_ref[1] != 0)
        def _():
            take(here_refs)

        @pl.when(place_ref[1] == 0)
        def _():
            take(there_refs)

        prepare_rows(chips, group, x_scr, undo_ref, y_scr, lhs_scr, undo_scr)

    rows = here * group
    lhs = lhs_scr[:, pl.ds(pl.multiple_of(step * rows, rows), rows), :].reshape(
        chips * rows, lhs_scr.shape[2]
    )
    for d in range(2):
        for bp in range(half // 2):
            lane = (d * half + 2 * bp) * zc
            t = jnp.dot(lhs, w_ref[:, lane : lane + 2 * zc], preferred_element_type=F32)
            t = t.reshape(chips * here, group, 2 * zc)
            t = jnp.concatenate([t[:, :, :zc], t[:, :, zc:]], axis=1).astype(BF16)
            t = t.reshape(chips, here, 2 * group, zc)
            for g in range(here):
                for q in range(chips):
                    k = q * part + bp * 2 * group
                    t_scr[d, g // 2, k : k + 2 * group, (g % 2) * zc : (g % 2 + 1) * zc] = t[q, g]
    for p in range(here // 2):
        for d in range(2):
            z_scr[d, p] = jnp.dot(col_scr[d], t_scr[d, p], preferred_element_type=F32)
    for g in range(here):
        lanes = slice((g % 2) * zc, (g % 2 + 1) * zc)
        undo = [undo_scr[d, pl.ds(step * here + g, 1), :] for d in range(2)]
        forward = z_scr[0, g // 2, :, lanes] * undo[0] + b_out_ref[...]
        mirror = z_scr[1, g // 2, :, lanes] * undo[1] + b_out_ref[...]
        pair = jnp.maximum(forward, 0.0) + jnp.maximum(mirror, 0.0)
        normed = norm_rows(pair, gain_ref[...], bias_ref[...]).astype(BF16)
        hidden = jnp.dot(normed, w_up_ref[...], preferred_element_type=F32) + b_up_ref[...]
        hidden = jnp.maximum(hidden, 0.0).astype(BF16)
        update = jnp.dot(hidden, w_down_ref[...], preferred_element_type=F32)
        out_ref[g] = (pair + update + b_down_ref[...]).astype(BF16)


def pair_kernel(place, group, rows_here, rows_there, cols, rest):
    own = cols[0]
    _, column_length, part = own.shape
    chips = (len(cols) + 1) // 2
    row_length = rows_here[0].shape[2]
    zc = rest[2].shape[1]
    here = math.gcd(row_length, 8)
    depth = chips * part
    lanes = 4 * part // group

    return pl.pallas_call(
        functools.partial(pair_body, chips, here, group, len(rows_here)),
        grid=(row_length // here,),
        in_specs=[pl.BlockSpec(memory_space=pltpu.SMEM)]
        + [whole(a) for a in (*rows_here, *rows_there, *cols, *rest)],
        out_specs=pl.BlockSpec((here, column_length, zc), lambda i: (i, 0, 0)),
        out_shape=jax.ShapeDtypeStruct((row_length, column_length, zc), BF16),
        scratch_shapes=[
            pltpu.VMEM((2, column_length, depth), BF16),
            pltpu.VMEM((2, chips * row_length, part), BF16),
            pltpu.VMEM((2, chips * row_length * group, lanes), F32),
            pltpu.VMEM((chips, row_length * group, 2 * lanes), F8),
            pltpu.VMEM((2, row_length, zc), F32),
            pltpu.VMEM((2, here // 2, depth, 2 * zc), BF16),
            pltpu.VMEM((2, here // 2, column_length, 2 * zc), F32),
        ],
        compiler_params=pltpu.CompilerParams(vmem_limit_bytes=56 << 20),
    )(place, *rows_here, *rows_there, *cols, *rest)


def ring_order(chips):
    return list(range(0, chips, 2)) + list(range(chips - 1, 0, -2))


def ring_source(chips, steps):
    order = ring_order(chips)
    place = {q: i for i, q in enumerate(order)}
    return [
        2 * order[(place[r // 2] + (steps if r % 2 else -steps)) % chips] + r % 2
        for r in range(2 * chips)
    ]


def shards(
    alignment,
    alignment_norm_gain,
    alignment_norm_bias,
    projection_weight,
    projection_bias_pair,
    w_out,
    b_out,
    pair_gain,
    pair_bias,
    w_up,
    b_up,
    w_down,
    b_down,
):
    local, column_length, _ = alignment.shape
    width = projection_weight.shape[1]
    half = width // 2
    row_count = lax.axis_size("row")
    col_count = lax.axis_size("col")
    row_length = column_length * col_count // row_count
    chips = row_count // 2
    row_index = lax.axis_index("row")
    col_index = lax.axis_index("col")
    core = row_index % 2

    def swap(a):
        return lax.ppermute(a, "row", [(r, r ^ 1) for r in range(row_count)])

    ring = [(src, r) for r, src in enumerate(ring_source(chips, 1))]

    mine = project(
        core.reshape(1),
        alignment,
        alignment_norm_gain[None],
        alignment_norm_bias[None],
        projection_weight.T,
        projection_bias_pair[None],
    )
    own = mine + swap(mine)

    per_col = column_length // row_length
    start = (row_index % per_col) * row_length
    source = row_index // per_col

    def cut(pieces, first):
        return jnp.stack(
            [
                jnp.stack([lax.dynamic_slice_in_dim(c, first, row_length, 0) for c in pair])
                for pair in pieces
            ]
        )

    def exchange(pieces):
        block = cut(pieces, start)
        if col_count == 2:
            return block, lax.ppermute(block, "col", [(0, 1), (1, 0)])
        block = lax.dynamic_index_in_dim(lax.all_gather(block, "col"), source, 0, False)
        return block, block

    right, left = own[0], own[1]
    cols = [own]
    early = [(right, left)]
    steps = chips // 2 - 1

    def direct(hops):
        sources = ring_source(chips, hops)
        targets = [sources.index(r) for r in range(row_count)]
        first = jnp.array([t % per_col * row_length for t in targets], jnp.int32)[row_index]
        pairs = [(2 * r + t // per_col, 2 * t + 1 - t // per_col) for r, t in enumerate(targets)]
        return lax.ppermute(cut([(right, left)], first), ("row", "col"), pairs)

    if col_count == 2:
        straight = [direct(steps), direct(-steps), direct(steps + 1)]
    rows = []
    for d in range(steps):
        right = lax.ppermute(right, "row", ring)
        left = lax.ppermute(left, "row", ring)
        pieces = [(right, left), (swap(right), swap(left))]
        for pair in pieces:
            cols.extend(pair)
        if d < steps - 1:
            early.extend(pieces)
        if d == steps - 2:
            rows.append(exchange(early))
        if d == steps - 1:
            params = (w_out, b_out, pair_gain, pair_bias, w_up, b_up, w_down, b_down)
            *params, right, left = lax.optimization_barrier((*params, right, left))
    far = lax.ppermute(jnp.where(core == 0, right, left), "row", ring)
    far_other = swap(far)
    cols.extend([far, far_other])
    a = lax.dynamic_slice_in_dim(far, start, row_length, 0)
    b = lax.dynamic_slice_in_dim(far_other, start, row_length, 0)
    far_pair = (jnp.where(core == 0, a, b), jnp.where(core == 0, b, a))
    pieces = pieces + [far_pair]
    last = cut(pieces[:2], start)
    if col_count == 2:
        rows.extend([(last[:1], straight[0]), (last[1:], straight[1])])
        rows.append((jnp.stack(far_pair)[None], straight[2]))
    else:
        last = jnp.concatenate([last, jnp.stack(far_pair)[None]])
        block = lax.dynamic_index_in_dim(lax.all_gather(last, "col"), source, 0, False)
        rows.append((block, block))

    group = 2 * local
    w_out, b_out, pair_gain, pair_bias, w_up, b_up, w_down, b_down = params
    w8, undo = split_weight(w_out, half, group * chips)
    rest = (w8, undo, b_out[None], pair_gain[None], pair_bias[None], w_up, b_up[None], w_down)
    place = jnp.stack([core, (source == col_index).astype(core.dtype)])
    return pair_kernel(
        place, group, [r[0] for r in rows], [r[1] for r in rows], cols, rest + (b_down[None],)
    )


def solution(mesh):
    return jax.shard_map(
        shards,
        mesh=mesh,
        in_specs=(P("row", "col", None),) + (P(),) * 12,
        out_specs=P("row", "col", None),
        check_vma=False,
    )
```

```python
import functools
import math

import jax
import jax.numpy as jnp
from jax import lax
from jax.experimental import pallas as pl
from jax.experimental.pallas import tpu as pltpu
from jax.sharding import PartitionSpec as P

EPSILON = 1e-05
F32 = jnp.float32
BF16 = jnp.bfloat16
F8 = jnp.float8_e4m3fn


def norm_rows(values, gain, bias):
    average = jnp.mean(values, axis=-1, keepdims=True)
    centered = values - average
    variance = jnp.mean(centered * centered, axis=-1, keepdims=True)
    return centered * lax.rsqrt(variance + EPSILON) * gain + bias


def project_body(core_ref, *refs):
    x_ref, gain_ref, bias_ref, weight_ref, pbias_ref = refs[6:11]
    out_ref, sems = refs[5], refs[11]
    copies = [pltpu.make_async_copy(refs[i], refs[6 + i], sems.at[i]) for i in range(5)]
    for copy in copies:
        copy.start()
    for copy in copies:
        copy.wait()
    local, _, _ = x_ref.shape
    width = weight_ref.shape[0]
    group = 2 * local
    lanes = width * group
    first = core_ref[0] * local
    ch = lax.rem(lax.broadcasted_iota(jnp.int32, (width, lanes), 0) + width // 2, width)
    lane = lax.broadcasted_iota(jnp.int32, (width, lanes), 1)
    total = None
    for s in range(local):
        normed = norm_rows(x_ref[s].astype(F32), gain_ref[...], bias_ref[...]).astype(BF16)
        y = lax.dot_general(
            normed, weight_ref[...], (((1,), (1,)), ((), ())), preferred_element_type=F32
        )
        y = y + pbias_ref[...]
        spread = (lane == ch * group + (first + s)).astype(F32).astype(BF16)
        part = jnp.dot(y.astype(BF16), spread, preferred_element_type=F32)
        total = part if total is None else total + part
    half = lanes // 2
    out_ref[0] = total[:, :half].astype(BF16)
    out_ref[1] = total[:, half:].astype(BF16)


def whole(a):
    return pl.BlockSpec(a.shape, lambda i: (0,) * len(a.shape))


def project(core, x, gain, bias, weight, pbias):
    local, residues, _ = x.shape
    lanes = weight.shape[0] * local
    operands = (x, gain, bias, weight, pbias)
    return pl.pallas_call(
        project_body,
        in_specs=[pl.BlockSpec(memory_space=pltpu.SMEM)]
        + [pl.BlockSpec(memory_space=pltpu.HBM)] * 5,
        out_specs=pl.BlockSpec(memory_space=pltpu.VMEM),
        out_shape=jax.ShapeDtypeStruct((2, residues, lanes), BF16),
        scratch_shapes=[pltpu.VMEM(a.shape, a.dtype) for a in operands]
        + [pltpu.SemaphoreType.DMA((5,))],
        compiler_params=pltpu.CompilerParams(vmem_limit_bytes=32 << 20),
    )(core, *operands)


def power_of_two(largest):
    scale = jnp.ones_like(largest)
    inverse = jnp.ones_like(largest)
    for k in (32, 16, 8, 4, 2, 1):
        fits = largest * (scale * float(2**k)) <= 448.0
        scale = jnp.where(fits, scale * float(2**k), scale)
        inverse = jnp.where(fits, inverse * float(2.0**-k), inverse)
    return scale, inverse


def split_weight(total, w_ref, w8_ref, undo_ref, scr):
    half = w8_ref.shape[0] // 8
    zc = w_ref.shape[1]
    scr[...] = w_ref[...].astype(F32)
    scale, inverse = power_of_two(jnp.max(jnp.abs(scr[...]), axis=0, keepdims=True))
    undo_ref[...] = inverse * (1.0 / total)
    zero = jnp.zeros((4 * half, half * zc), w8_ref.dtype)
    w8_ref[4 * half :, : half * zc] = zero
    w8_ref[: 4 * half, half * zc :] = zero
    for d in range(2):
        for k in range(half):
            if d == 0:
                block = scr[pl.ds(k, half, stride=half), :]
            else:
                block = scr[k * half : (k + 1) * half, :]
            block = block * scale
            high = block.astype(w8_ref.dtype)
            low = (block - high.astype(F32)).astype(w8_ref.dtype)
            lanes = slice((d * half + k) * zc, (d * half + k + 1) * zc)
            row = d * 4 * half
            w8_ref[row : row + half, lanes] = high
            w8_ref[row + half : row + 2 * half, lanes] = high
            w8_ref[row + 2 * half : row + 3 * half, lanes] = low
            w8_ref[row + 3 * half : row + 4 * half, lanes] = low


def prepare_rows(chips, group, x_scr, undo_ref, y_scr, lhs_scr, undo_scr):
    row_length = x_scr.shape[1] // chips
    part = x_scr.shape[2]
    half = part // group
    lanes = 4 * half
    k = lax.broadcasted_iota(jnp.int32, (part, lanes), 0)
    lane = lax.broadcasted_iota(jnp.int32, (part, lanes), 1)
    offset = k - lax.rem(lane, half) * group
    count = chips * row_length
    for side in range(2):
        x = x_scr[1 - side]
        for s in range(group):
            pick = jnp.where(offset == s, 1.0, 0.0).astype(BF16)
            y_scr[side, pl.ds(s, count, stride=group), :] = jnp.dot(
                x, pick, preferred_element_type=F32
            )
        largest = None
        for q in range(chips):
            y = y_scr[side, q * row_length * group : (q + 1) * row_length * group, :]
            m = jnp.max(jnp.abs(y).reshape(row_length, group, lanes), axis=1)
            largest = m if largest is None else jnp.maximum(largest, m)
        largest = jnp.max(largest, axis=-1, keepdims=True)
        scale, inverse = power_of_two(jnp.broadcast_to(largest, (row_length, lanes)))
        undo_scr[side] = inverse * undo_ref[...]
        spread = jnp.broadcast_to(scale[:, None, :], (row_length, group, lanes)).reshape(
            row_length * group, lanes
        )
        here = lax.broadcasted_iota(jnp.int32, (row_length * group, lanes), 1)
        is_high = lax.rem(lax.div(here, half), 2) == 0
        for q in range(chips):
            y = y_scr[side, q * row_length * group : (q + 1) * row_length * group, :] * spread
            high = y.astype(F8).astype(F32)
            both = jnp.where(is_high, high, y - high).astype(F8)
            lhs_scr[q, :, side * lanes : (side + 1) * lanes] = both


def pair_body(chips, here, group, row_parts, place_ref, *refs):
    there_refs = refs[:row_parts]
    refs = refs[row_parts:]
    own_ref, *col_refs = refs[: chips * 2 - 1]
    (w_out_ref, b_out_ref, gain_ref, bias_ref, w_up_ref, b_up_ref, w_down_ref, b_down_ref) = (
        refs[chips * 2 - 1 : chips * 2 + 7]
    )
    out_ref, col_scr, x_scr, y_scr, lhs_scr, undo_scr, t_scr, z_scr, w_ref, undo_ref, w_scr = refs[chips * 2 + 7 :]
    part = own_ref.shape[2]
    zc = out_ref.shape[2]
    half = part // group
    step = pl.program_id(0)

    @pl.when(step == 0)
    def _():
        for d in range(2):
            col_scr[d, :, :part] = own_ref[d]
            for q in range(1, chips - 1):
                col_scr[d, :, q * part : (q + 1) * part] = col_refs[2 * (q - 1) + d][...]

        far = slice((chips - 1) * part, chips * part)
        far_here, far_there = col_refs[-2:]

        @pl.when(place_ref[0] == 0)
        def _():
            col_scr[0, :, far] = far_here[...]
            col_scr[1, :, far] = far_there[...]

        @pl.when(place_ref[0] != 0)
        def _():
            col_scr[0, :, far] = far_there[...]
            col_scr[1, :, far] = far_here[...]

        row_length = x_scr.shape[1] // chips

        @pl.when(place_ref[1] != 0)
        def _():
            first = pl.multiple_of(place_ref[2] * row_length, row_length)
            for side in range(2):
                for q in range(chips):
                    x_scr[side, q * row_length : (q + 1) * row_length, :] = col_scr[
                        side, pl.ds(first, row_length), q * part : (q + 1) * part
                    ]

        @pl.when(place_ref[1] == 0)
        def _():
            blocks = [(r, q) for r in there_refs for q in range(r.shape[0])]
            for i, (r, q) in enumerate(blocks):
                for side in range(2):
                    x_scr[side, i * row_length : (i + 1) * row_length, :] = r[q, side]

        split_weight(chips * group, w_out_ref, w_ref, undo_ref, w_scr)
        prepare_rows(chips, group, x_scr, undo_ref, y_scr, lhs_scr, undo_scr)

    rows = here * group
    lhs = lhs_scr[:, pl.ds(pl.multiple_of(step * rows, rows), rows), :].reshape(
        chips * rows, lhs_scr.shape[2]
    )
    for d in range(2):
        for bp in range(half // 2):
            lane = (d * half + 2 * bp) * zc
            t = jnp.dot(lhs, w_ref[:, lane : lane + 2 * zc], preferred_element_type=F32)
            t = t.reshape(chips * here, group, 2 * zc)
            t = jnp.concatenate([t[:, :, :zc], t[:, :, zc:]], axis=1).astype(BF16)
            t = t.reshape(chips, here, 2 * group, zc)
            for g in range(here):
                for q in range(chips):
                    k = q * part + bp * 2 * group
                    t_scr[d, g // 2, k : k + 2 * group, (g % 2) * zc : (g % 2 + 1) * zc] = t[q, g]
    for p in range(here // 2):
        for d in range(2):
            z_scr[d, p] = jnp.dot(col_scr[d], t_scr[d, p], preferred_element_type=F32)
    for g in range(here):
        lanes = slice((g % 2) * zc, (g % 2 + 1) * zc)
        undo = [undo_scr[d, pl.ds(step * here + g, 1), :] for d in range(2)]
        forward = z_scr[0, g // 2, :, lanes] * undo[0] + b_out_ref[...]
        mirror = z_scr[1, g // 2, :, lanes] * undo[1] + b_out_ref[...]
        pair = jnp.maximum(forward, 0.0) + jnp.maximum(mirror, 0.0)
        normed = norm_rows(pair, gain_ref[...], bias_ref[...]).astype(BF16)
        hidden = jnp.dot(normed, w_up_ref[...], preferred_element_type=F32) + b_up_ref[...]
        hidden = jnp.maximum(hidden, 0.0).astype(BF16)
        update = jnp.dot(hidden, w_down_ref[...], preferred_element_type=F32)
        out_ref[g] = (pair + update + b_down_ref[...]).astype(BF16)


def pair_kernel(place, group, rows, cols, rest):
    own = cols[0]
    _, column_length, part = own.shape
    chips = (len(cols) + 1) // 2
    row_length = rows[0].shape[2]
    zc = rest[1].shape[1]
    here = math.gcd(row_length, 8)
    depth = chips * part
    lanes = 4 * part // group

    return pl.pallas_call(
        functools.partial(pair_body, chips, here, group, len(rows)),
        grid=(row_length // here,),
        in_specs=[pl.BlockSpec(memory_space=pltpu.SMEM)]
        + [whole(a) for a in (*rows, *cols, *rest)],
        out_specs=pl.BlockSpec((here, column_length, zc), lambda i: (i, 0, 0)),
        out_shape=jax.ShapeDtypeStruct((row_length, column_length, zc), BF16),
        scratch_shapes=[
            pltpu.VMEM((2, column_length, depth), BF16),
            pltpu.VMEM((2, chips * row_length, part), BF16),
            pltpu.VMEM((2, chips * row_length * group, lanes), F32),
            pltpu.VMEM((chips, row_length * group, 2 * lanes), F8),
            pltpu.VMEM((2, row_length, zc), F32),
            pltpu.VMEM((2, here // 2, depth, 2 * zc), BF16),
            pltpu.VMEM((2, here // 2, column_length, 2 * zc), F32),
            pltpu.VMEM((2 * lanes, 2 * part // group * zc), F8),
            pltpu.VMEM((1, zc), F32),
            pltpu.VMEM(rest[0].shape, F32),
        ],
        compiler_params=pltpu.CompilerParams(vmem_limit_bytes=56 << 20),
    )(place, *rows, *cols, *rest)


def ring_order(chips):
    return list(range(0, chips, 2)) + list(range(chips - 1, 0, -2))


def ring_source(chips):
    order = ring_order(chips)
    place = {q: i for i, q in enumerate(order)}
    return [
        2 * order[(place[r // 2] + (1 if r % 2 else -1)) % chips] + r % 2
        for r in range(2 * chips)
    ]


def shards(
    alignment,
    alignment_norm_gain,
    alignment_norm_bias,
    projection_weight,
    projection_bias_pair,
    w_out,
    b_out,
    pair_gain,
    pair_bias,
    w_up,
    b_up,
    w_down,
    b_down,
):
    local, column_length, _ = alignment.shape
    width = projection_weight.shape[1]
    half = width // 2
    row_count = lax.axis_size("row")
    col_count = lax.axis_size("col")
    row_length = column_length * col_count // row_count
    chips = row_count // 2
    row_index = lax.axis_index("row")
    col_index = lax.axis_index("col")
    core = row_index % 2

    def swap(a):
        return lax.ppermute(a, "row", [(r, r ^ 1) for r in range(row_count)])

    ring = [(src, r) for r, src in enumerate(ring_source(chips))]

    mine = project(
        core.reshape(1),
        alignment,
        alignment_norm_gain[None],
        alignment_norm_bias[None],
        projection_weight.T,
        projection_bias_pair[None],
    )
    own = mine + swap(mine)

    per_col = column_length // row_length
    start = (row_index % per_col) * row_length
    source = row_index // per_col

    def cut(pair, first, count):
        return jnp.stack([lax.dynamic_slice_in_dim(c, first, count, 0) for c in pair])

    def across(block):
        return lax.ppermute(block, "col", [(0, 1), (1, 0)])

    right, left = own[0], own[1]
    cols = [own]
    steps = chips // 2 - 1
    two = col_count == 2
    if two:
        targets = [row_count - 2 - r + 2 * (r % 2) for r in range(row_count)]
        first = (row_count - 2 - row_index + 2 * core) % per_col * row_length
        far_rows = lax.ppermute(
            lax.dynamic_slice_in_dim(own, first, row_length, 1),
            ("row", "col"),
            [(2 * r + t // per_col, 2 * t + 1 - t // per_col) for r, t in enumerate(targets)],
        )
    blocks = [cut((right, left), start, row_length)]
    for d in range(steps):
        right = lax.ppermute(right, "row", ring)
        left = lax.ppermute(left, "row", ring)
        other = (swap(right), swap(left))
        cols.extend([right, left, *other])
        if d < steps - 1 or not two:
            blocks.extend([cut(pair, start, row_length) for pair in ((right, left), other)])
        if d == steps - 2 and two:
            rows = [across(jnp.stack(blocks))]
    far = lax.ppermute(jnp.where(core == 0, right, left), "row", ring)
    if two:
        both = across(cut((right, left), start - core * row_length, 2 * row_length))
        far, both = lax.optimization_barrier((far, both))
        kept = lax.dynamic_slice_in_dim(both, core * row_length, row_length, 1)
        given = lax.dynamic_slice_in_dim(both, (1 - core) * row_length, row_length, 1)
        rows.extend([kept[None], swap(given)[None], far_rows[None]])
    far_other = swap(far)
    cols.extend([far, far_other])
    is_here = (source == col_index).astype(core.dtype)
    if not two:
        a = lax.dynamic_slice_in_dim(far, start, row_length, 0)
        b = lax.dynamic_slice_in_dim(far_other, start, row_length, 0)
        blocks.append(jnp.stack([jnp.where(core == 0, a, b), jnp.where(core == 0, b, a)]))
        gathered = lax.all_gather(jnp.stack(blocks), "col")
        rows = [lax.dynamic_index_in_dim(gathered, source, 0, False)]
        is_here = jnp.zeros_like(is_here)

    place = jnp.stack([core, is_here, row_index % per_col])
    rest = (w_out, b_out[None], pair_gain[None], pair_bias[None], w_up, b_up[None], w_down)
    return pair_kernel(place, 2 * local, rows, cols, rest + (b_down[None],))


def solution(mesh):
    return jax.shard_map(
        shards,
        mesh=mesh,
        in_specs=(P("row", "col", None),) + (P(),) * 12,
        out_specs=P("row", "col", None),
        check_vma=False,
    )
```

```python
import functools
import math

import jax
import jax.numpy as jnp
from jax import lax
from jax.experimental import pallas as pl
from jax.experimental.pallas import tpu as pltpu
from jax.sharding import PartitionSpec as P

EPSILON = 1e-05
F32 = jnp.float32
BF16 = jnp.bfloat16
F8 = jnp.float8_e4m3fn


def norm_rows(values, gain, bias):
    average = jnp.mean(values, axis=-1, keepdims=True)
    centered = values - average
    variance = jnp.mean(centered * centered, axis=-1, keepdims=True)
    return centered * lax.rsqrt(variance + EPSILON) * gain + bias


def project_body(place_ref, x_ref, packed_ref, out_ref):
    local = x_ref.shape[0]
    width = packed_ref.shape[0] - 3
    weight = packed_ref[:width, :].astype(BF16)
    gain = packed_ref[width : width + 1, :]
    bias = packed_ref[width + 1 : width + 2, :]
    pbias = packed_ref[width + 2 :, :width]
    group = 2 * local
    lanes = width * group
    first = place_ref[0] * local
    ch = lax.rem(lax.broadcasted_iota(jnp.int32, (width, lanes), 0) + width // 2, width)
    lane = lax.broadcasted_iota(jnp.int32, (width, lanes), 1)
    total = None
    for s in range(local):
        normed = norm_rows(x_ref[s].astype(F32), gain, bias).astype(BF16)
        y = lax.dot_general(
            normed, weight, (((1,), (1,)), ((), ())), preferred_element_type=F32
        )
        y = y + pbias
        spread = (lane == ch * group + (first + s)).astype(F32).astype(BF16)
        part = jnp.dot(y.astype(BF16), spread, preferred_element_type=F32)
        total = part if total is None else total + part
    half = lanes // 2
    out_ref[0] = total[:, :half].astype(BF16)
    out_ref[1] = total[:, half:].astype(BF16)


def whole(a):
    return pl.BlockSpec(a.shape, lambda i: (0,) * len(a.shape))


def project(place, x, packed):
    local, residues, _ = x.shape
    lanes = (packed.shape[0] - 3) * local
    vmem = pl.BlockSpec(memory_space=pltpu.VMEM)
    return pl.pallas_call(
        project_body,
        in_specs=[pl.BlockSpec(memory_space=pltpu.SMEM), vmem, vmem],
        out_specs=vmem,
        out_shape=jax.ShapeDtypeStruct((2, residues, lanes), BF16),
        compiler_params=pltpu.CompilerParams(vmem_limit_bytes=32 << 20),
    )(place, x, packed)


def power_of_two(largest):
    scale = jnp.ones_like(largest)
    inverse = jnp.ones_like(largest)
    for k in (32, 16, 8, 4, 2, 1):
        fits = largest * (scale * float(2**k)) <= 448.0
        scale = jnp.where(fits, scale * float(2**k), scale)
        inverse = jnp.where(fits, inverse * float(2.0**-k), inverse)
    return scale, inverse


def split_weight(total, w_ref, w8_ref, undo_ref, scr):
    half = w8_ref.shape[0] // 8
    zc = w_ref.shape[1]
    scr[...] = w_ref[...].astype(F32)
    scale, inverse = power_of_two(jnp.max(jnp.abs(scr[...]), axis=0, keepdims=True))
    undo_ref[...] = inverse * (1.0 / total)
    zero = jnp.zeros((4 * half, half * zc), w8_ref.dtype)
    w8_ref[4 * half :, : half * zc] = zero
    w8_ref[: 4 * half, half * zc :] = zero
    for d in range(2):
        for k in range(half):
            if d == 0:
                block = scr[pl.ds(k, half, stride=half), :]
            else:
                block = scr[k * half : (k + 1) * half, :]
            block = block * scale
            high = block.astype(w8_ref.dtype)
            low = (block - high.astype(F32)).astype(w8_ref.dtype)
            lanes = slice((d * half + k) * zc, (d * half + k + 1) * zc)
            row = d * 4 * half
            w8_ref[row : row + half, lanes] = high
            w8_ref[row + half : row + 2 * half, lanes] = high
            w8_ref[row + 2 * half : row + 3 * half, lanes] = low
            w8_ref[row + 3 * half : row + 4 * half, lanes] = low


def prepare_rows(chips, group, x_scr, undo_ref, y_scr, lhs_scr, undo_scr):
    row_length = x_scr.shape[1] // chips
    part = x_scr.shape[2]
    half = part // group
    lanes = 4 * half
    k = lax.broadcasted_iota(jnp.int32, (part, lanes), 0)
    lane = lax.broadcasted_iota(jnp.int32, (part, lanes), 1)
    offset = k - lax.rem(lane, half) * group
    count = chips * row_length
    for side in range(2):
        x = x_scr[1 - side]
        for s in range(group):
            pick = jnp.where(offset == s, 1.0, 0.0).astype(BF16)
            y_scr[side, pl.ds(s, count, stride=group), :] = jnp.dot(
                x, pick, preferred_element_type=F32
            )
        largest = None
        for q in range(chips):
            y = y_scr[side, q * row_length * group : (q + 1) * row_length * group, :]
            m = jnp.max(jnp.abs(y).reshape(row_length, group, lanes), axis=1)
            largest = m if largest is None else jnp.maximum(largest, m)
        largest = jnp.max(largest, axis=-1, keepdims=True)
        scale, inverse = power_of_two(jnp.broadcast_to(largest, (row_length, lanes)))
        undo_scr[side] = inverse * undo_ref[...]
        spread = jnp.broadcast_to(scale[:, None, :], (row_length, group, lanes)).reshape(
            row_length * group, lanes
        )
        here = lax.broadcasted_iota(jnp.int32, (row_length * group, lanes), 1)
        is_high = lax.rem(lax.div(here, half), 2) == 0
        for q in range(chips):
            y = y_scr[side, q * row_length * group : (q + 1) * row_length * group, :] * spread
            high = y.astype(F8).astype(F32)
            both = jnp.where(is_high, high, y - high).astype(F8)
            lhs_scr[q, :, side * lanes : (side + 1) * lanes] = both


def pair_body(chips, here, group, row_parts, place_ref, *refs):
    there_refs = refs[:row_parts]
    refs = refs[row_parts:]
    own_ref, *col_refs = refs[: chips * 2 - 1]
    (w_out_ref, b_out_ref, gain_ref, bias_ref, w_up_ref, b_up_ref, w_down_ref, b_down_ref) = (
        refs[chips * 2 - 1 : chips * 2 + 7]
    )
    out_ref, col_scr, x_scr, y_scr, lhs_scr, undo_scr, t_scr, z_scr, w_ref, undo_ref, w_scr = refs[chips * 2 + 7 :]
    part = own_ref.shape[2]
    zc = out_ref.shape[2]
    half = part // group
    step = pl.program_id(0)

    @pl.when(step == 0)
    def _():
        for d in range(2):
            col_scr[d, :, :part] = own_ref[d]
            for q in range(1, chips - 1):
                col_scr[d, :, q * part : (q + 1) * part] = col_refs[2 * (q - 1) + d][...]

        far = slice((chips - 1) * part, chips * part)
        far_here, far_there = col_refs[-2:]

        @pl.when(place_ref[0] == 0)
        def _():
            col_scr[0, :, far] = far_here[...]
            col_scr[1, :, far] = far_there[...]

        @pl.when(place_ref[0] != 0)
        def _():
            col_scr[0, :, far] = far_there[...]
            col_scr[1, :, far] = far_here[...]

        row_length = x_scr.shape[1] // chips

        @pl.when(place_ref[1] != 0)
        def _():
            first = pl.multiple_of(place_ref[2] * row_length, row_length)
            for side in range(2):
                for q in range(chips):
                    x_scr[side, q * row_length : (q + 1) * row_length, :] = col_scr[
                        side, pl.ds(first, row_length), q * part : (q + 1) * part
                    ]

        @pl.when(place_ref[1] == 0)
        def _():
            blocks = []
            for r in there_refs:
                if len(r.shape) == 4:
                    blocks.extend((r.at[q], 0) for q in range(r.shape[0]))
                elif r.shape[1] == row_length:
                    blocks.append((r, 0))
                else:
                    skip = r.shape[1] - 2 * row_length
                    if skip and not blocks:
                        blocks.append((r, 0))
                    skip = skip + place_ref[0] * row_length
                    blocks.append((r, pl.multiple_of(skip, row_length)))
            for i, (r, skip) in enumerate(blocks):
                for side in range(2):
                    x_scr[side, i * row_length : (i + 1) * row_length, :] = r[
                        side, pl.ds(skip, row_length), :
                    ]

        split_weight(chips * group, w_out_ref, w_ref, undo_ref, w_scr)
        prepare_rows(chips, group, x_scr, undo_ref, y_scr, lhs_scr, undo_scr)

    rows = here * group
    lhs = lhs_scr[:, pl.ds(pl.multiple_of(step * rows, rows), rows), :].reshape(
        chips * rows, lhs_scr.shape[2]
    )
    for d in range(2):
        for bp in range(half // 2):
            lane = (d * half + 2 * bp) * zc
            t = jnp.dot(lhs, w_ref[:, lane : lane + 2 * zc], preferred_element_type=F32)
            t = t.reshape(chips * here, group, 2 * zc)
            t = jnp.concatenate([t[:, :, :zc], t[:, :, zc:]], axis=1).astype(BF16)
            t = t.reshape(chips, here, 2 * group, zc)
            for g in range(here):
                for q in range(chips):
                    k = q * part + bp * 2 * group
                    t_scr[d, g // 2, k : k + 2 * group, (g % 2) * zc : (g % 2 + 1) * zc] = t[q, g]
    for p in range(here // 2):
        for d in range(2):
            z_scr[d, p] = jnp.dot(col_scr[d], t_scr[d, p], preferred_element_type=F32)
    for g in range(here):
        lanes = slice((g % 2) * zc, (g % 2 + 1) * zc)
        undo = [undo_scr[d, pl.ds(step * here + g, 1), :] for d in range(2)]
        forward = z_scr[0, g // 2, :, lanes] * undo[0] + b_out_ref[...]
        mirror = z_scr[1, g // 2, :, lanes] * undo[1] + b_out_ref[...]
        pair = jnp.maximum(forward, 0.0) + jnp.maximum(mirror, 0.0)
        normed = norm_rows(pair, gain_ref[...], bias_ref[...]).astype(BF16)
        hidden = jnp.dot(normed, w_up_ref[...], preferred_element_type=F32) + b_up_ref[...]
        hidden = jnp.maximum(hidden, 0.0).astype(BF16)
        update = jnp.dot(hidden, w_down_ref[...], preferred_element_type=F32)
        out_ref[g] = (pair + update + b_down_ref[...]).astype(BF16)


def pair_kernel(place, group, row_length, rows, cols, rest):
    own = cols[0]
    _, column_length, part = own.shape
    chips = (len(cols) + 1) // 2
    zc = rest[1].shape[1]
    here = math.gcd(row_length, 8)
    depth = chips * part
    lanes = 4 * part // group

    return pl.pallas_call(
        functools.partial(pair_body, chips, here, group, len(rows)),
        grid=(row_length // here,),
        in_specs=[pl.BlockSpec(memory_space=pltpu.SMEM)]
        + [whole(a) for a in (*rows, *cols, *rest)],
        out_specs=pl.BlockSpec((here, column_length, zc), lambda i: (i, 0, 0)),
        out_shape=jax.ShapeDtypeStruct((row_length, column_length, zc), BF16),
        scratch_shapes=[
            pltpu.VMEM((2, column_length, depth), BF16),
            pltpu.VMEM((2, chips * row_length, part), BF16),
            pltpu.VMEM((2, chips * row_length * group, lanes), F32),
            pltpu.VMEM((chips, row_length * group, 2 * lanes), F8),
            pltpu.VMEM((2, row_length, zc), F32),
            pltpu.VMEM((2, here // 2, depth, 2 * zc), BF16),
            pltpu.VMEM((2, here // 2, column_length, 2 * zc), F32),
            pltpu.VMEM((2 * lanes, 2 * part // group * zc), F8),
            pltpu.VMEM((1, zc), F32),
            pltpu.VMEM(rest[0].shape, F32),
        ],
        compiler_params=pltpu.CompilerParams(vmem_limit_bytes=56 << 20),
    )(place, *rows, *cols, *rest)


def ring_order(chips):
    return list(range(0, chips, 2)) + list(range(chips - 1, 0, -2))


def ring_source(chips):
    order = ring_order(chips)
    place = {q: i for i, q in enumerate(order)}
    return [
        2 * order[(place[r // 2] + (1 if r % 2 else -1)) % chips] + r % 2
        for r in range(2 * chips)
    ]


def shards(
    alignment,
    alignment_norm_gain,
    alignment_norm_bias,
    projection_weight,
    projection_bias_pair,
    w_out,
    b_out,
    pair_gain,
    pair_bias,
    w_up,
    b_up,
    w_down,
    b_down,
):
    local, column_length, _ = alignment.shape
    width = projection_weight.shape[1]
    half = width // 2
    row_count = lax.axis_size("row")
    col_count = lax.axis_size("col")
    row_length = column_length * col_count // row_count
    chips = row_count // 2
    row_index = lax.axis_index("row")
    col_index = lax.axis_index("col")
    core = row_index % 2

    def swap(a):
        return lax.ppermute(a, "row", [(r, r ^ 1) for r in range(row_count)])

    ring = [(src, r) for r, src in enumerate(ring_source(chips))]

    per_col = column_length // row_length
    source = row_index // per_col
    is_here = (source == col_index).astype(core.dtype)
    if col_count != 2:
        is_here = jnp.zeros_like(is_here)
    place = jnp.stack([core, is_here, row_index % per_col])
    pad = jnp.pad(projection_bias_pair, (0, alignment_norm_gain.shape[0] - width))
    packed = jnp.concatenate(
        [
            projection_weight.T.astype(F32),
            jnp.stack([alignment_norm_gain, alignment_norm_bias, pad]),
        ]
    )
    mine = project(place, alignment, packed)
    own = mine + swap(mine)

    start = (row_index % per_col) * row_length

    def cut(pair, first, count):
        return jnp.stack([lax.dynamic_slice_in_dim(c, first, count, 0) for c in pair])

    def across(block):
        return lax.ppermute(block, "col", [(0, 1), (1, 0)])

    right, left = own[0], own[1]
    cols = [own]
    steps = chips // 2 - 1
    two = col_count == 2
    if two:
        targets = [row_count - 2 - r + 2 * (r % 2) for r in range(row_count)]
        first = (row_count - 2 - row_index + 2 * core) % per_col * row_length
        far_rows = lax.ppermute(
            lax.dynamic_slice_in_dim(own, first, row_length, 1),
            ("row", "col"),
            [(2 * r + t // per_col, 2 * t + 1 - t // per_col) for r, t in enumerate(targets)],
        )
    blocks = [cut((right, left), start, row_length)]
    rows = []
    both = None
    pair_start = start - core * row_length
    for d in range(steps):
        right = lax.ppermute(right, "row", ring)
        left = lax.ppermute(left, "row", ring)
        if two:
            if d > 0:
                right, left, both = lax.optimization_barrier((right, left, both))
                rows.extend([both, swap(both)])
            both = cut((right, left), pair_start, 2 * row_length)
            if d == 0:
                both = jnp.concatenate([blocks[0], both], axis=1)
            both = across(both)
        other = (swap(right), swap(left))
        cols.extend([right, left, *other])
        if not two:
            blocks.extend([cut(pair, start, row_length) for pair in ((right, left), other)])
    far = lax.ppermute(jnp.where(core == 0, right, left), "row", ring)
    if two:
        far, both = lax.optimization_barrier((far, both))
        rows.extend([both, swap(both), far_rows])
    far_other = swap(far)
    cols.extend([far, far_other])
    if not two:
        a = lax.dynamic_slice_in_dim(far, start, row_length, 0)
        b = lax.dynamic_slice_in_dim(far_other, start, row_length, 0)
        blocks.append(jnp.stack([jnp.where(core == 0, a, b), jnp.where(core == 0, b, a)]))
        gathered = lax.all_gather(jnp.stack(blocks), "col")
        rows = [lax.dynamic_index_in_dim(gathered, source, 0, False)]

    rest = (w_out, b_out[None], pair_gain[None], pair_bias[None], w_up, b_up[None], w_down)
    return pair_kernel(place, 2 * local, row_length, rows, cols, rest + (b_down[None],))


def solution(mesh):
    return jax.shard_map(
        shards,
        mesh=mesh,
        in_specs=(P("row", "col", None),) + (P(),) * 12,
        out_specs=P("row", "col", None),
        check_vma=False,
    )
```

```python
import functools
import math

import jax
import jax.numpy as jnp
from jax import lax
from jax.experimental import pallas as pl
from jax.experimental.pallas import tpu as pltpu
from jax.sharding import PartitionSpec as P

EPSILON = 1e-05
F32 = jnp.float32
BF16 = jnp.bfloat16
F8 = jnp.float8_e4m3fn


def norm_rows(values, gain, bias):
    average = jnp.mean(values, axis=-1, keepdims=True)
    centered = values - average
    variance = jnp.mean(centered * centered, axis=-1, keepdims=True)
    return centered * lax.rsqrt(variance + EPSILON) * gain + bias


def project_body(core_ref, *refs):
    x_ref, weight_ref, vectors_ref, out_ref = refs
    local, _, channels = x_ref.shape
    width = weight_ref.shape[0]
    gain = vectors_ref[:, :channels]
    bias = vectors_ref[:, channels : 2 * channels]
    pbias = vectors_ref[:, 2 * channels :]
    group = 2 * local
    lanes = width * group
    first = core_ref[0] * local
    ch = lax.rem(lax.broadcasted_iota(jnp.int32, (width, lanes), 0) + width // 2, width)
    lane = lax.broadcasted_iota(jnp.int32, (width, lanes), 1)
    total = None
    for s in range(local):
        normed = norm_rows(x_ref[s].astype(F32), gain, bias).astype(BF16)
        y = lax.dot_general(
            normed, weight_ref[...], (((1,), (1,)), ((), ())), preferred_element_type=F32
        )
        y = y + pbias
        spread = (lane == ch * group + (first + s)).astype(F32).astype(BF16)
        part = jnp.dot(y.astype(BF16), spread, preferred_element_type=F32)
        total = part if total is None else total + part
    half = lanes // 2
    out_ref[0] = total[:, :half].astype(BF16)
    out_ref[1] = total[:, half:].astype(BF16)


def whole(a):
    return pl.BlockSpec(a.shape, lambda i: (0,) * len(a.shape))


def project(core, x, weight, vectors):
    local, residues, _ = x.shape
    lanes = weight.shape[0] * local
    vmem = pl.BlockSpec(memory_space=pltpu.VMEM)
    return pl.pallas_call(
        project_body,
        in_specs=[pl.BlockSpec(memory_space=pltpu.SMEM)] + [vmem] * 3,
        out_specs=vmem,
        out_shape=jax.ShapeDtypeStruct((2, residues, lanes), BF16),
        compiler_params=pltpu.CompilerParams(vmem_limit_bytes=32 << 20),
    )(core, x, weight, vectors)


def power_of_two(largest):
    scale = jnp.ones_like(largest)
    inverse = jnp.ones_like(largest)
    for k in (32, 16, 8, 4, 2, 1):
        fits = largest * (scale * float(2**k)) <= 448.0
        scale = jnp.where(fits, scale * float(2**k), scale)
        inverse = jnp.where(fits, inverse * float(2.0**-k), inverse)
    return scale, inverse


def split_weight(total, w_ref, w8_ref, undo_ref, scr):
    half = w8_ref.shape[0] // 8
    zc = w_ref.shape[1]
    scr[...] = w_ref[...].astype(F32)
    scale, inverse = power_of_two(jnp.max(jnp.abs(scr[...]), axis=0, keepdims=True))
    undo_ref[...] = inverse * (1.0 / total)
    zero = jnp.zeros((4 * half, half * zc), w8_ref.dtype)
    w8_ref[4 * half :, : half * zc] = zero
    w8_ref[: 4 * half, half * zc :] = zero
    for d in range(2):
        for k in range(half):
            if d == 0:
                block = scr[pl.ds(k, half, stride=half), :]
            else:
                block = scr[k * half : (k + 1) * half, :]
            block = block * scale
            high = block.astype(w8_ref.dtype)
            low = (block - high.astype(F32)).astype(w8_ref.dtype)
            lanes = slice((d * half + k) * zc, (d * half + k + 1) * zc)
            row = d * 4 * half
            w8_ref[row : row + half, lanes] = high
            w8_ref[row + half : row + 2 * half, lanes] = high
            w8_ref[row + 2 * half : row + 3 * half, lanes] = low
            w8_ref[row + 3 * half : row + 4 * half, lanes] = low


def prepare_rows(chips, group, x_scr, undo_ref, y_scr, lhs_scr, undo_scr):
    row_length = x_scr.shape[1] // chips
    part = x_scr.shape[2]
    half = part // group
    lanes = 4 * half
    k = lax.broadcasted_iota(jnp.int32, (part, lanes), 0)
    lane = lax.broadcasted_iota(jnp.int32, (part, lanes), 1)
    offset = k - lax.rem(lane, half) * group
    count = chips * row_length
    for side in range(2):
        x = x_scr[1 - side]
        for s in range(group):
            pick = jnp.where(offset == s, 1.0, 0.0).astype(BF16)
            y_scr[side, pl.ds(s, count, stride=group), :] = jnp.dot(
                x, pick, preferred_element_type=F32
            )
        largest = None
        for q in range(chips):
            y = y_scr[side, q * row_length * group : (q + 1) * row_length * group, :]
            m = jnp.max(jnp.abs(y).reshape(row_length, group, lanes), axis=1)
            largest = m if largest is None else jnp.maximum(largest, m)
        largest = jnp.max(largest, axis=-1, keepdims=True)
        scale, inverse = power_of_two(jnp.broadcast_to(largest, (row_length, lanes)))
        undo_scr[side] = inverse * undo_ref[...]
        spread = jnp.broadcast_to(scale[:, None, :], (row_length, group, lanes)).reshape(
            row_length * group, lanes
        )
        here = lax.broadcasted_iota(jnp.int32, (row_length * group, lanes), 1)
        is_high = lax.rem(lax.div(here, half), 2) == 0
        for q in range(chips):
            y = y_scr[side, q * row_length * group : (q + 1) * row_length * group, :] * spread
            high = y.astype(F8).astype(F32)
            both = jnp.where(is_high, high, y - high).astype(F8)
            lhs_scr[q, :, side * lanes : (side + 1) * lanes] = both


def row_places(chips, refs, row_length):
    if len(refs) == 1:
        return [(refs[0].at[q], q, 0, False) for q in range(chips)]
    first, first_other, later, later_other, far = refs
    places = [(first, 0, 0, False)]
    for skip, pair in ((row_length, (first, first_other)), (0, (later, later_other))):
        for k in range((pair[0].shape[1] - skip) // (2 * row_length)):
            for r in pair:
                places.append((r, len(places), skip + 2 * k * row_length, True))
    return places + [(far, chips - 1, 0, False)]


def pair_body(chips, here, group, row_parts, place_ref, *refs):
    there_refs = refs[:row_parts]
    refs = refs[row_parts:]
    own_ref, *col_refs = refs[: chips * 2 - 1]
    (w_out_ref, b_out_ref, gain_ref, bias_ref, w_up_ref, b_up_ref, w_down_ref, b_down_ref) = (
        refs[chips * 2 - 1 : chips * 2 + 7]
    )
    out_ref, col_scr, x_scr, y_scr, lhs_scr, undo_scr, t_scr, z_scr, w_ref, undo_ref, w_scr = refs[chips * 2 + 7 :]
    part = own_ref.shape[2]
    zc = out_ref.shape[2]
    half = part // group
    step = pl.program_id(0)

    @pl.when(step == 0)
    def _():
        for d in range(2):
            col_scr[d, :, :part] = own_ref[d]
            for q in range(1, chips - 1):
                col_scr[d, :, q * part : (q + 1) * part] = col_refs[2 * (q - 1) + d][...]

        far = slice((chips - 1) * part, chips * part)
        far_here, far_there = col_refs[-2:]

        @pl.when(place_ref[0] == 0)
        def _():
            col_scr[0, :, far] = far_here[...]
            col_scr[1, :, far] = far_there[...]

        @pl.when(place_ref[0] != 0)
        def _():
            col_scr[0, :, far] = far_there[...]
            col_scr[1, :, far] = far_here[...]

        row_length = x_scr.shape[1] // chips

        @pl.when(place_ref[1] != 0)
        def _():
            first = pl.multiple_of(place_ref[2] * row_length, row_length)
            for side in range(2):
                for q in range(chips):
                    x_scr[side, q * row_length : (q + 1) * row_length, :] = col_scr[
                        side, pl.ds(first, row_length), q * part : (q + 1) * part
                    ]

        @pl.when(place_ref[1] == 0)
        def _():
            for r, i, skip, core_rows in row_places(chips, there_refs, row_length):
                if core_rows:
                    skip = pl.multiple_of(skip + place_ref[0] * row_length, row_length)
                for side in range(2):
                    x_scr[side, i * row_length : (i + 1) * row_length, :] = r[
                        side, pl.ds(skip, row_length), :
                    ]

        split_weight(chips * group, w_out_ref, w_ref, undo_ref, w_scr)
        prepare_rows(chips, group, x_scr, undo_ref, y_scr, lhs_scr, undo_scr)

    rows = here * group
    lhs = lhs_scr[:, pl.ds(pl.multiple_of(step * rows, rows), rows), :].reshape(
        chips * rows, lhs_scr.shape[2]
    )
    for d in range(2):
        for bp in range(half // 2):
            lane = (d * half + 2 * bp) * zc
            t = jnp.dot(lhs, w_ref[:, lane : lane + 2 * zc], preferred_element_type=F32)
            t = t.reshape(chips * here, group, 2 * zc)
            t = jnp.concatenate([t[:, :, :zc], t[:, :, zc:]], axis=1).astype(BF16)
            t = t.reshape(chips, here, 2 * group, zc)
            for g in range(here):
                for q in range(chips):
                    k = q * part + bp * 2 * group
                    t_scr[d, g // 2, k : k + 2 * group, (g % 2) * zc : (g % 2 + 1) * zc] = t[q, g]
    for p in range(here // 2):
        for d in range(2):
            z_scr[d, p] = jnp.dot(col_scr[d], t_scr[d, p], preferred_element_type=F32)
    for g in range(here):
        lanes = slice((g % 2) * zc, (g % 2 + 1) * zc)
        undo = [undo_scr[d, pl.ds(step * here + g, 1), :] for d in range(2)]
        forward = z_scr[0, g // 2, :, lanes] * undo[0] + b_out_ref[...]
        mirror = z_scr[1, g // 2, :, lanes] * undo[1] + b_out_ref[...]
        pair = jnp.maximum(forward, 0.0) + jnp.maximum(mirror, 0.0)
        normed = norm_rows(pair, gain_ref[...], bias_ref[...]).astype(BF16)
        hidden = jnp.dot(normed, w_up_ref[...], preferred_element_type=F32) + b_up_ref[...]
        hidden = jnp.maximum(hidden, 0.0).astype(BF16)
        update = jnp.dot(hidden, w_down_ref[...], preferred_element_type=F32)
        out_ref[g] = (pair + update + b_down_ref[...]).astype(BF16)


def pair_kernel(place, group, row_length, rows, cols, rest):
    own = cols[0]
    _, column_length, part = own.shape
    chips = (len(cols) + 1) // 2
    zc = rest[1].shape[1]
    here = math.gcd(row_length, 8)
    depth = chips * part
    lanes = 4 * part // group

    return pl.pallas_call(
        functools.partial(pair_body, chips, here, group, len(rows)),
        grid=(row_length // here,),
        in_specs=[pl.BlockSpec(memory_space=pltpu.SMEM)]
        + [whole(a) for a in (*rows, *cols, *rest)],
        out_specs=pl.BlockSpec((here, column_length, zc), lambda i: (i, 0, 0)),
        out_shape=jax.ShapeDtypeStruct((row_length, column_length, zc), BF16),
        scratch_shapes=[
            pltpu.VMEM((2, column_length, depth), BF16),
            pltpu.VMEM((2, chips * row_length, part), BF16),
            pltpu.VMEM((2, chips * row_length * group, lanes), F32),
            pltpu.VMEM((chips, row_length * group, 2 * lanes), F8),
            pltpu.VMEM((2, row_length, zc), F32),
            pltpu.VMEM((2, here // 2, depth, 2 * zc), BF16),
            pltpu.VMEM((2, here // 2, column_length, 2 * zc), F32),
            pltpu.VMEM((2 * lanes, 2 * part // group * zc), F8),
            pltpu.VMEM((1, zc), F32),
            pltpu.VMEM(rest[0].shape, F32),
        ],
        compiler_params=pltpu.CompilerParams(vmem_limit_bytes=56 << 20),
    )(place, *rows, *cols, *rest)


def ring_order(chips):
    return list(range(0, chips, 2)) + list(range(chips - 1, 0, -2))


def ring_source(chips):
    order = ring_order(chips)
    place = {q: i for i, q in enumerate(order)}
    return [
        2 * order[(place[r // 2] + (1 if r % 2 else -1)) % chips] + r % 2
        for r in range(2 * chips)
    ]


def shards(
    alignment,
    alignment_norm_gain,
    alignment_norm_bias,
    projection_weight,
    projection_bias_pair,
    w_out,
    b_out,
    pair_gain,
    pair_bias,
    w_up,
    b_up,
    w_down,
    b_down,
):
    local, column_length, _ = alignment.shape
    width = projection_weight.shape[1]
    half = width // 2
    row_count = lax.axis_size("row")
    col_count = lax.axis_size("col")
    row_length = column_length * col_count // row_count
    chips = row_count // 2
    row_index = lax.axis_index("row")
    col_index = lax.axis_index("col")
    core = row_index % 2

    def swap(a):
        return lax.ppermute(a, "row", [(r, r ^ 1) for r in range(row_count)])

    ring = [(src, r) for r, src in enumerate(ring_source(chips))]

    vectors = jnp.concatenate([alignment_norm_gain, alignment_norm_bias, projection_bias_pair])
    mine = project(core.reshape(1), alignment, projection_weight.T, vectors[None])
    own = mine + swap(mine)

    per_col = column_length // row_length
    start = (row_index % per_col) * row_length
    source = row_index // per_col

    def cut(pair, first, count):
        return jnp.stack([lax.dynamic_slice_in_dim(c, first, count, 0) for c in pair])

    def across(block):
        return lax.ppermute(block, "col", [(0, 1), (1, 0)])

    right, left = own[0], own[1]
    cols = [own]
    steps = chips // 2 - 1
    two = col_count == 2
    is_here = (source == col_index).astype(core.dtype) if two else jnp.zeros_like(core)
    place = jnp.stack([core, is_here, row_index % per_col])
    if two:
        targets = [row_count - 2 - r + 2 * (r % 2) for r in range(row_count)]
        first = (row_count - 2 - row_index + 2 * core) % per_col * row_length
        far_rows = lax.ppermute(
            lax.dynamic_slice_in_dim(own, first, row_length, 1),
            ("row", "col"),
            [(2 * r + t // per_col, 2 * t + 1 - t // per_col) for r, t in enumerate(targets)],
        )
    blocks = [cut((right, left), start, row_length)]
    later = []
    pair_start = start - core * row_length
    for d in range(steps):
        right = lax.ppermute(right, "row", ring)
        left = lax.ppermute(left, "row", ring)
        if two:
            if d == 1:
                right, left, far_rows, place = lax.optimization_barrier(
                    (right, left, far_rows, place)
                )
            if d == steps - 1 and d > 1:
                right, left, early = lax.optimization_barrier((right, left, early))
            both = cut((right, left), pair_start, 2 * row_length)
            later.append(both)
            if d == steps - 2:
                early = across(jnp.concatenate([blocks[0], *later], axis=1))
                later = []
        other = (swap(right), swap(left))
        cols.extend([right, left, *other])
        if not two:
            blocks.extend([cut(pair, start, row_length) for pair in ((right, left), other)])
    far = lax.ppermute(jnp.where(core == 0, right, left), "row", ring)
    if two:
        late = across(jnp.concatenate(later, axis=1))
        early_other = swap(early)
        far, late, early_other = lax.optimization_barrier((far, late, early_other))
        rows = [early, early_other, late, swap(late), far_rows]
    far_other = swap(far)
    cols.extend([far, far_other])
    if not two:
        a = lax.dynamic_slice_in_dim(far, start, row_length, 0)
        b = lax.dynamic_slice_in_dim(far_other, start, row_length, 0)
        blocks.append(jnp.stack([jnp.where(core == 0, a, b), jnp.where(core == 0, b, a)]))
        gathered = lax.all_gather(jnp.stack(blocks), "col")
        rows = [lax.dynamic_index_in_dim(gathered, source, 0, False)]
    rest = (w_out, b_out[None], pair_gain[None], pair_bias[None], w_up, b_up[None], w_down)
    return pair_kernel(place, 2 * local, row_length, rows, cols, rest + (b_down[None],))


def solution(mesh):
    return jax.shard_map(
        shards,
        mesh=mesh,
        in_specs=(P("row", "col", None),) + (P(),) * 12,
        out_specs=P("row", "col", None),
        check_vma=False,
    )
```
